32 devices in a mesh: src: 8 (over z, y), tgt: 4 (over x, core).
Axes of the slice: x: 2, y: 2, z: 4, core: 2. Of those that a mesh axis runs over, the one named last changes fastest.
Arguments:
- edge_state: bfloat16 [8, 4, 1024, 512], P('src', 'tgt'), may hold values from -6 to 6
- edge_source: int32 [8, 4, 1024], P('src', 'tgt'), may hold values from 0 to 255
- edge_target: int32 [8, 4, 1024], P('src', 'tgt'), may hold values from 0 to 511
- live_edges: int32 [8, 4], P('src', 'tgt'), may hold values from 64 to 1024, as said below
- inner_one: bfloat16 [512, 512], replicated, may hold values from -0.25 to 0.25
- outer_one: bfloat16 [512, 512], replicated, may hold values from -0.25 to 0.25
- inner_two: bfloat16 [512, 512], replicated, may hold values from -0.25 to 0.25
- outer_two: bfloat16 [512, 512], replicated, may hold values from -0.25 to 0.25
- gain_one: float32 [512], replicated, may hold values from 0.1 to 1.9
- gain_two: float32 [512], replicated, may hold values from 0.1 to 1.9
Outputs:
- final_state: bfloat16 [8, 4, 1024, 512], P('src', 'tgt')
The draws below stay inside these ranges and needn't reach their ends.
Inputs may be any that keep to these rules, and one draw needn't show every extreme that they name: `edge_source`: source atoms within a block. `edge_target`: target atoms within a block. `live_edges`: a multiple of 64; some block pair is full in every draw.
All inputs are finite; a program needn't handle non-finite values.
Results may differ from the reference program's by a relative error of at most 0.013.
Values sent between devices are 32-bit elements; how exact they have to be, the bound alone decides.
No kernel may reach another device: no remote copies, remote signals or barrier semaphores. Data moves between devices by JAX's collectives and lax.ppermute only.
A program may use at most 64 MiB of HBM per device.

```python
import jax
import jax.numpy as jnp
from jax import lax

C = 512
E_DEV = 1024
SRC_ATOMS = 256
TGT_ATOMS = 512
ATOMS = 2048
N_SRC = 8
N_TGT = 4


def draw_live_edges(key, part):
    key_steps, key_full = jax.random.split(key)
    multiples = jax.random.randint(key_steps, (N_SRC * N_TGT,), 1, 17)
    counts = E_DEV // 16 * multiples
    fullest = jax.random.randint(key_full, (), 0, N_SRC * N_TGT)
    counts = counts.at[fullest].set(E_DEV)
    return counts.reshape(N_SRC, N_TGT).astype(jnp.int32)


def set_ends(entries, rng, low, largest):
    spot = [jax.random.randint(jax.random.fold_in(rng, axis), (), 0, length) for axis, length in enumerate(entries.shape)]
    longest = entries.shape.index(max(entries.shape))
    next_to = spot[:longest] + [(spot[longest] + 1) % entries.shape[longest]] + spot[longest + 1:]
    return entries.at[tuple(spot)].set(low).at[tuple(next_to)].set(largest)


def levels(own_key, shape, cuts, least, largest):
    loudness = 1.0
    for dim, shards_of in cuts:
        draws = jax.random.uniform(jax.random.fold_in(jax.random.fold_in(own_key, 6), dim), (shards_of,), jnp.float32, least / len(cuts), largest / len(cuts))
        loudness = loudness * jnp.repeat(jnp.exp(draws), shape[dim] // shards_of).reshape((-1,) + (1,) * (len(shape) - 1 - dim))
    return loudness


def noise(key, shape, width, most, shards=(), kind=jnp.bfloat16):
    array = width * jax.random.normal(key, shape, jnp.float32)
    if shards:
        array = array * levels(key, shape, shards, -0.22, 0.18)
    return jnp.clip(array, -most, most).astype(kind)


def setup_inputs(seed: int = 0) -> dict:
    keys = jax.random.split(jax.random.key(seed), 11)
    edge_state = noise(keys[0], (N_SRC, N_TGT, E_DEV, C), 1.0, 6.0, ((0, 8), (1, 4)))
    edge_source = set_ends(jax.random.randint(keys[1], (N_SRC, N_TGT, E_DEV), 0, SRC_ATOMS), jax.random.fold_in(keys[1], 1), 0, SRC_ATOMS - 1).astype(jnp.int32)
    edge_target = set_ends(jax.random.randint(keys[2], (N_SRC, N_TGT, E_DEV), 0, TGT_ATOMS), jax.random.fold_in(keys[2], 1), 0, TGT_ATOMS - 1).astype(jnp.int32)
    live_edges = draw_live_edges(jax.random.fold_in(keys[10], 71), 0)
    inner_one = noise(keys[4], (C, C), C ** -0.5, 0.25)
    outer_one = noise(keys[5], (C, C), C ** -0.5, 0.25)
    inner_two = noise(keys[6], (C, C), C ** -0.5, 0.25)
    outer_two = noise(keys[7], (C, C), C ** -0.5, 0.25)
    gain_one = jnp.clip(1.0 + 0.18 * jax.random.normal(keys[8], (C,), jnp.float32), 0.1, 1.9)
    gain_two = jnp.clip(1.0 + 0.18 * jax.random.normal(keys[9], (C,), jnp.float32), 0.1, 1.9)
    return {"edge_state": edge_state, "edge_source": edge_source, "edge_target": edge_target, "live_edges": live_edges, "inner_one": inner_one, "outer_one": outer_one, "inner_two": inner_two, "outer_two": outer_two, "gain_one": gain_one, "gain_two": gain_two}


def update_edges(message, inner, outer, gain):
    mean_square = lax.optimization_barrier(jnp.mean(message * message, axis=-1, keepdims=True))
    normed = message * lax.rsqrt(mean_square + 1e-05) * gain.astype(jnp.float32)
    normed_low = normed.astype(jnp.bfloat16)
    activated = jax.nn.relu(jnp.dot(normed_low, inner, preferred_element_type=jnp.float32)).astype(jnp.bfloat16)
    return normed + jnp.dot(activated, outer, preferred_element_type=jnp.float32)

def reference(edge_state, edge_source, edge_target, live_edges, inner_one, outer_one, inner_two, outer_two, gain_one, gain_two):
    src_blocks, tgt_blocks, edge_rows, channels = edge_state.shape
    total_atoms = ATOMS
    alive = jnp.arange(edge_rows)[None, None, :] < live_edges[:, :, None]
    source_atom = edge_source + (jnp.arange(src_blocks) * SRC_ATOMS)[:, None, None].astype(edge_source.dtype)
    target_atom = edge_target + (jnp.arange(tgt_blocks) * TGT_ATOMS)[None, :, None].astype(edge_target.dtype)

    def accumulate(running, inputs):
        values, atom_index, keep_rows = inputs
        contributions = jnp.where(keep_rows[..., None], values.astype(jnp.float32), jnp.float32(0.0))
        added = jax.ops.segment_sum(contributions.reshape(-1, channels), atom_index.reshape(-1), num_segments=total_atoms)
        return (running + added, None)
    empty = jnp.zeros((total_atoms, channels), jnp.float32)
    incoming, _ = lax.scan(accumulate, empty, (edge_state, target_atom, alive))

    def layer_one(inputs):
        values, atom_index, keep_rows = inputs
        message = incoming[atom_index] - values.astype(jnp.float32)
        result = update_edges(message, inner_one, outer_one, gain_one)
        return jnp.where(keep_rows[..., None], result, jnp.float32(0.0)).astype(jnp.bfloat16)
    reverse_state = lax.map(layer_one, (edge_state, target_atom, alive))
    outgoing, _ = lax.scan(accumulate, empty, (reverse_state, source_atom, alive))

    def layer_two(inputs):
        values, atom_index, keep_rows = inputs
        message = outgoing[atom_index] - values.astype(jnp.float32)
        result = update_edges(message, inner_two, outer_two, gain_two)
        return jnp.where(keep_rows[..., None], result, jnp.float32(0.0)).astype(jnp.bfloat16)
    return lax.map(layer_two, (reverse_state, source_atom, alive))
```

```python
import functools

import jax
import jax.numpy as jnp
from jax import lax
from jax.experimental import pallas as pl
from jax.experimental.pallas import tpu as pltpu
from jax.sharding import PartitionSpec as P

ATOM_DEV = 64
GROUP = 4
WAVES = 2
ROW_BLOCK = 256
VMEM_LIMIT = 40 * 1024 * 1024

VMEM = pl.BlockSpec(memory_space=pltpu.VMEM)
SMEM = pl.BlockSpec(memory_space=pltpu.SMEM)


def call(kernel, out_shape, n_smem, n_vmem, flops, bytes_accessed, scratch=()):
    return pl.pallas_call(
        kernel,
        out_shape=out_shape,
        in_specs=[SMEM] * n_smem + [VMEM] * n_vmem,
        out_specs=jax.tree.map(lambda _: VMEM, out_shape),
        scratch_shapes=list(scratch),
        compiler_params=pltpu.CompilerParams(vmem_limit_bytes=VMEM_LIMIT),
        cost_estimate=pl.CostEstimate(flops=flops, bytes_accessed=bytes_accessed, transcendentals=0),
    )


def target_sum_kernel(first, flip_ref, live_ref, target_ref, state_ref, *chunk_refs):
    rows = target_ref.shape[1]
    size = chunk_refs[0].shape[0]
    count = size * len(chunk_refs)
    place = jnp.bitwise_xor(target_ref[...], flip_ref[0])
    place = jnp.where(lax.broadcasted_iota(jnp.int32, (1, rows), 1) < live_ref[0], place, -1)
    slot = lax.broadcasted_iota(jnp.int32, (count, rows), 0) + first
    chosen = jnp.where(place == slot, jnp.float32(1.0), jnp.float32(0.0)).astype(jnp.bfloat16)
    for index, chunk_ref in enumerate(chunk_refs):
        chunk_ref[...] = jnp.dot(
            chosen[index * size : (index + 1) * size], state_ref[...], preferred_element_type=jnp.float32
        )


def target_sums(states, targets, flip, live, wave, size):
    rows, channels = states.shape
    out = [jax.ShapeDtypeStruct((size, channels), jnp.float32)] * GROUP
    return call(
        functools.partial(target_sum_kernel, wave * size * GROUP),
        out, 2, 2,
        2 * size * GROUP * rows * channels, 2 * rows * channels + 4 * size * GROUP * channels,
    )(flip, live, targets, states)


def split_sums(sum_refs, parts_ref):
    total = parts_ref.shape[0] // 3
    at = 0
    for sum_ref in sum_refs:
        size = sum_ref.shape[0]
        value = sum_ref[...]
        for part in range(3):
            low = value.astype(jnp.bfloat16)
            parts_ref[part * total + at : part * total + at + size, :] = low
            value = value - low.astype(jnp.float32)
        at += size


def update_block(chosen, parts_ref, state, live, first_row, inner_ref, outer_ref, gain_ref):
    gathered = jnp.dot(
        jnp.concatenate([chosen, chosen, chosen], axis=1), parts_ref[...], preferred_element_type=jnp.float32
    )
    message = gathered - state.astype(jnp.float32)
    mean_square = jnp.mean(message * message, axis=-1, keepdims=True)
    normed = message * lax.rsqrt(mean_square + 1e-05) * gain_ref[...]
    activated = jax.nn.relu(
        jnp.dot(normed.astype(jnp.bfloat16), inner_ref[...], preferred_element_type=jnp.float32)
    ).astype(jnp.bfloat16)
    result = normed + jnp.dot(activated, outer_ref[...], preferred_element_type=jnp.float32)
    row = lax.broadcasted_iota(jnp.int32, (state.shape[0], 1), 0) + first_row
    return jnp.where(row < live, result, jnp.float32(0.0)).astype(jnp.bfloat16)


def layer_one_kernel(n_sums, live_ref, *refs):
    sum_refs = refs[:n_sums]
    chosen_ref, source_ref, state_ref, inner_ref, outer_ref, gain_ref, reverse_ref, own_ref, other_ref, parts_ref = refs[n_sums:]
    split_sums(sum_refs, parts_ref)
    rows = state_ref.shape[0]
    half = own_ref.shape[0]
    live = live_ref[0]
    total = None
    for first_row in range(0, rows, ROW_BLOCK):
        block = slice(first_row, first_row + ROW_BLOCK)
        low = update_block(
            chosen_ref[block, :], parts_ref, state_ref[block, :], live, first_row, inner_ref, outer_ref, gain_ref
        )
        reverse_ref[block, :] = low
        term = jnp.dot(source_ref[:, block], low, preferred_element_type=jnp.float32)
        total = term if total is None else total + term
    own_ref[...] = total[:half]
    other_ref[...] = total[half:]


def layer_two_kernel(live_ref, own_ref, other_ref, chosen_ref, state_ref, inner_ref, outer_ref, gain_ref, final_ref, parts_ref):
    split_sums((own_ref, other_ref), parts_ref)
    rows = state_ref.shape[0]
    live = live_ref[0]
    for first_row in range(0, rows, ROW_BLOCK):
        block = slice(first_row, first_row + ROW_BLOCK)
        final_ref[block, :] = update_block(
            chosen_ref[block, :], parts_ref, state_ref[block, :], live, first_row, inner_ref, outer_ref, gain_ref
        )


def swap(value, axis, mask):
    return lax.ppermute(value, axis, [(i, i ^ mask) for i in range(lax.axis_size(axis))])


def higher_masks(axis, low):
    masks = []
    while low < lax.axis_size(axis):
        masks.append(low)
        low *= 2
    return masks


def spread(total, axis):
    return [total] + [swap(total, axis, mask) for mask in range(1, GROUP)]


def target_totals(waves):
    received = [[swap(chunks[mask], "src", mask) for mask in range(1, GROUP)] for chunks in waves]
    sums = []
    for chunks, parts in zip(waves, received):
        if sums:
            parts, _ = lax.optimization_barrier((parts, sums[-1]))
        sums.append(chunks[0] + parts[0] + parts[1] + parts[2])
    for mask in higher_masks("src", GROUP):
        sums = [value + swap(value, "src", mask) for value in sums]
    return [chunk for value in sums for chunk in spread(value, "src")]


def source_totals(own, other):
    own = own + swap(other, "tgt", 1)
    for mask in higher_masks("tgt", 2):
        own = own + swap(own, "tgt", mask)
    return own, swap(own, "tgt", 1)


def body(
    edge_state,
    edge_source,
    edge_target,
    live_edges,
    inner_one,
    outer_one,
    inner_two,
    outer_two,
    gain_one,
    gain_two,
):
    rows, channels = edge_state.shape[2:]
    states = edge_state.reshape(rows, channels)
    sources = edge_source.reshape(1, rows)
    targets = edge_target.reshape(1, rows)
    live = live_edges.reshape(1)
    target_atoms = ATOM_DEV * lax.axis_size("src")
    source_atoms = ATOM_DEV * lax.axis_size("tgt")
    size = target_atoms // (GROUP * WAVES)
    half = source_atoms // 2
    target_flip = lax.bitwise_and(lax.axis_index("src"), GROUP - 1) * size
    source_flip = lax.bitwise_and(lax.axis_index("tgt"), 1) * half

    waves = [target_sums(states, targets, target_flip.reshape(1), live, wave, size) for wave in range(WAVES)]

    def chosen(values, flip, count):
        place = jnp.bitwise_xor(values.reshape(rows, 1), flip)
        return (place == lax.broadcasted_iota(jnp.int32, (rows, count), 1)).astype(jnp.bfloat16)

    target_chosen = chosen(targets, target_flip, target_atoms)
    source_chosen = chosen(sources, source_flip, source_atoms)
    source_place = jnp.bitwise_xor(sources, source_flip)
    source_pick = (source_place == lax.broadcasted_iota(jnp.int32, (source_atoms, rows), 0)).astype(jnp.bfloat16)

    totals = target_totals(waves)
    reverse_state, own, other = call(
        functools.partial(layer_one_kernel, len(totals)),
        [
            jax.ShapeDtypeStruct((rows, channels), jnp.bfloat16),
            jax.ShapeDtypeStruct((half, channels), jnp.float32),
            jax.ShapeDtypeStruct((half, channels), jnp.float32),
        ],
        1, len(totals) + 6,
        2 * rows * channels * (3 * target_atoms + 2 * channels + source_atoms), 8 * rows * channels,
        [pltpu.VMEM((3 * target_atoms, channels), jnp.bfloat16)],
    )(live, *totals, target_chosen, source_pick, states, inner_one, outer_one, gain_one.reshape(1, channels))
    own, other = source_totals(own, other)
    final_state = call(
        layer_two_kernel,
        jax.ShapeDtypeStruct((rows, channels), jnp.bfloat16),
        1, 7,
        2 * rows * channels * (3 * source_atoms + 2 * channels), 8 * rows * channels,
        [pltpu.VMEM((3 * source_atoms, channels), jnp.bfloat16)],
    )(live, own, other, source_chosen, reverse_state, inner_two, outer_two, gain_two.reshape(1, channels))
    return final_state.reshape(1, 1, rows, channels)


def solution(mesh):
    placed = (
        P("src", "tgt", None, None),
        P("src", "tgt", None),
        P("src", "tgt", None),
        P("src", "tgt"),
        P(),
        P(),
        P(),
        P(),
        P(),
        P(),
    )
    return jax.shard_map(
        body, mesh=mesh, in_specs=placed, out_specs=P("src", "tgt", None, None), check_vma=False
    )
```

```python
import functools

import jax
import jax.numpy as jnp
from jax import lax
from jax.experimental import pallas as pl
from jax.experimental.pallas import tpu as pltpu
from jax.sharding import PartitionSpec as P

ATOM_DEV = 64
GROUP = 4
MASKS = (0, 2, 1, 3)
SHARES = (4, 4)
REDUCE_STEPWISE = (False, False)
SPREAD_STEPWISE = (True, False)
PIECES = 2
LANES = 128
HIDE_FLOPS = 8 * 10**9
VMEM_LIMIT = 40 * 1024 * 1024
FIRST_VMEM_LIMIT = 52 * 1024 * 1024

VMEM = pl.BlockSpec(memory_space=pltpu.VMEM)
HBM = pl.BlockSpec(memory_space=pltpu.HBM)


def call(kernel, out_shape, in_specs, flops, scratch=(), out_specs=None, limit=VMEM_LIMIT):
    return pl.pallas_call(
        kernel,
        out_shape=out_shape,
        in_specs=in_specs,
        out_specs=jax.tree.map(lambda _: VMEM, out_shape) if out_specs is None else out_specs,
        scratch_shapes=list(scratch),
        compiler_params=pltpu.CompilerParams(vmem_limit_bytes=limit),
        cost_estimate=pl.CostEstimate(flops=flops, bytes_accessed=0, transcendentals=0),
    )


def wave_sizes(atoms):
    return [atoms // (GROUP * sum(SHARES)) * share for share in SHARES]


def target_place(atoms, sizes):
    device = lax.axis_index("src")
    own = (device // 2) % 2 + (device % 2) * 2
    place = atoms
    base = 0
    for size in sizes:
        inside = atoms - base
        chunk = sum((inside >= k * size).astype(jnp.int32) for k in range(1, GROUP))
        spot = base + jnp.bitwise_xor(chunk, own) * size + inside - chunk * size
        place = jnp.where(inside >= 0, spot, place)
        base += GROUP * size
    return place


def source_place(atoms, half):
    return jnp.bitwise_xor(atoms, (lax.axis_index("tgt") % 2) * half)


def one_hot(place, slot):
    return jnp.where(place == slot, jnp.float32(1.0), jnp.float32(0.0)).astype(jnp.bfloat16)


def store_sums(wave, sizes, live, targets, fetch, chunk_refs):
    rows = targets.shape[1]
    size = sizes[wave]
    place = target_place(targets, sizes)
    place = jnp.where(lax.broadcasted_iota(jnp.int32, (1, rows), 1) < live, place, -1)
    slot = lax.broadcasted_iota(jnp.int32, (size * GROUP, rows), 0) + sum(sizes[:wave]) * GROUP
    chosen = one_hot(place, slot)
    states = fetch()
    at = 0
    for chunk_ref in chunk_refs:
        count = chunk_ref.shape[0]
        chunk_ref[...] = jnp.dot(chosen[at : at + count], states, preferred_element_type=jnp.float32)
        at += count


def first_sum_kernel(sizes, live_hbm, target_hbm, state_hbm, *refs):
    *chunk_refs, live_out, target_ref, state_ref, live_ref, sems = refs
    copies = [
        pltpu.make_async_copy(source, place, sems.at[index])
        for index, (source, place) in enumerate(((live_hbm, live_ref), (target_hbm, target_ref), (state_hbm, state_ref)))
    ]
    for copy in copies:
        copy.start()
    copies[0].wait()
    live = live_ref[0, 0]
    live_out[...] = jnp.full(live_out.shape, live, jnp.int32)
    copies[1].wait()

    def fetch():
        copies[2].wait()
        return state_ref[...]

    store_sums(0, sizes, live, target_ref[...], fetch, chunk_refs)


def later_sum_kernel(wave, sizes, live_ref, target_ref, state_ref, *chunk_refs):
    store_sums(wave, sizes, live_ref[:, :1], target_ref[...], lambda: state_ref[...], chunk_refs)


def chunk_shapes(wave, size, channels):
    counts = [size, size, 2 * size] if REDUCE_STEPWISE[wave] else [size] * GROUP
    return [jax.ShapeDtypeStruct((count, channels), jnp.float32) for count in counts]


def first_sums(states, targets, live, sizes):
    rows, channels = states.shape
    handed_on = [
        jax.ShapeDtypeStruct((1, LANES), jnp.int32),
        jax.ShapeDtypeStruct(targets.shape, targets.dtype),
        jax.ShapeDtypeStruct(states.shape, states.dtype),
    ]
    out = call(
        functools.partial(first_sum_kernel, sizes), chunk_shapes(0, sizes[0], channels) + handed_on, [HBM] * 3,
        2 * sizes[0] * GROUP * rows * channels,
        [pltpu.SMEM((1, 1), jnp.int32), pltpu.SemaphoreType.DMA((3,))],
        limit=FIRST_VMEM_LIMIT,
    )(live, targets, states)
    return out[:-3], *out[-3:]


def later_sums(states, targets, live, wave, sizes):
    rows, channels = states.shape
    return call(
        functools.partial(later_sum_kernel, wave, sizes), chunk_shapes(wave, sizes[wave], channels), [VMEM] * 3,
        2 * sizes[wave] * GROUP * rows * channels,
    )(live, targets, states)


def choose_kernel(sizes, half, target_ref, source_ref, tie_ref, target_chosen_ref, source_chosen_ref, source_pick_ref):
    del tie_ref
    rows = target_ref.shape[1]
    sources = source_place(source_ref[...], half)
    for values, chosen_ref in ((target_place(target_ref[...], sizes), target_chosen_ref), (sources, source_chosen_ref)):
        place = jnp.transpose(jnp.broadcast_to(values, (LANES, rows)))
        lane = lax.broadcasted_iota(jnp.int32, (rows, LANES), 1)
        for first in range(0, chosen_ref.shape[1], LANES):
            chosen_ref[:, first : first + LANES] = one_hot(place, lane + first)
    source_pick_ref[...] = one_hot(sources, lax.broadcasted_iota(jnp.int32, source_pick_ref.shape, 0))


def split_sums(sum_refs, parts_ref):
    total = parts_ref.shape[0] // 3
    at = 0
    for sum_ref in sum_refs:
        size = sum_ref.shape[0]
        value = sum_ref[...]
        for part in range(3):
            low = value.astype(jnp.bfloat16)
            parts_ref[part * total + at : part * total + at + size, :] = low
            value = value - low.astype(jnp.float32)
        at += size


def normed_activated(chosen_ref, parts_ref, state_ref, inner_ref, gain_ref):
    chosen = chosen_ref[...]
    gathered = jnp.dot(
        jnp.concatenate([chosen, chosen, chosen], axis=1), parts_ref[...], preferred_element_type=jnp.float32
    )
    message = gathered - state_ref[...].astype(jnp.float32)
    mean_square = jnp.mean(message * message, axis=-1, keepdims=True)
    normed = message * lax.rsqrt(mean_square + 1e-05) * gain_ref[...]
    activated = jax.nn.relu(
        jnp.dot(normed.astype(jnp.bfloat16), inner_ref[...], preferred_element_type=jnp.float32)
    ).astype(jnp.bfloat16)
    return normed, activated


def finish(normed, activated, outer_ref, live_ref, first_row):
    result = normed + jnp.dot(activated, outer_ref[...], preferred_element_type=jnp.float32)
    row = lax.broadcasted_iota(jnp.int32, (result.shape[0], 1), 0) + first_row
    return jnp.where(row < live_ref[:, :1], result, jnp.float32(0.0)).astype(jnp.bfloat16)


def layer_one_kernel(n_sums, live_ref, *refs):
    sum_refs = refs[:n_sums]
    chosen_ref, pick_ref, state_ref, inner_ref, outer_ref, gain_ref, reverse_ref, *piece_refs, parts_ref = refs[n_sums:]
    split_sums(sum_refs, parts_ref)
    normed, activated = normed_activated(chosen_ref, parts_ref, state_ref, inner_ref, gain_ref)
    reverse_ref[...] = finish(normed, activated, outer_ref, live_ref, 0)
    total = jnp.dot(pick_ref[...], reverse_ref[...], preferred_element_type=jnp.float32)
    size = piece_refs[0].shape[0]
    for index, piece_ref in enumerate(piece_refs):
        piece_ref[...] = total[index * size : (index + 1) * size]


def layer_two_kernel(n_sums, live_ref, *refs):
    sum_refs = refs[:n_sums]
    chosen_ref, state_ref, inner_ref, outer_ref, gain_ref, final_hbm, parts_ref, final_ref, sems = refs[n_sums:]
    split_sums(sum_refs, parts_ref)
    normed, activated = normed_activated(chosen_ref, parts_ref, state_ref, inner_ref, gain_ref)
    block = final_ref.shape[0] // 2
    copies = []
    for index in range(2):
        rows = pl.ds(index * block, block)
        part = slice(index * block, (index + 1) * block)
        final_ref[rows, :] = finish(normed[part], activated[part], outer_ref, live_ref, index * block)
        copies.append(pltpu.make_async_copy(final_ref.at[rows], final_hbm.at[rows], sems.at[index]))
        copies[-1].start()
    for copy in copies:
        copy.wait()


def swap(value, axis, mask):
    return lax.ppermute(value, axis, [(i, i ^ mask) for i in range(lax.axis_size(axis))])


def higher_masks(axis, low):
    masks = []
    while low < lax.axis_size(axis):
        masks.append(low)
        low *= 2
    return masks


def tie(value, other):
    return lax.optimization_barrier((value, other))[0]


def spread(total, stepwise):
    if not stepwise:
        return [total] + [swap(total, "src", mask) for mask in MASKS[1:]]
    second = swap(total, "src", MASKS[1])
    return [total, second, swap(jnp.concatenate([total, second]), "src", MASKS[2])]


def reduce(chunks, stepwise, ready):
    if not stepwise:
        parts = ready([swap(chunk, "src", mask) for chunk, mask in zip(chunks[1:], MASKS[1:])])
        return chunks[0] + parts[0] + parts[1] + parts[2]
    size = chunks[0].shape[0]
    part = swap(chunks[2], "src", MASKS[2])
    return chunks[0] + part[:size] + ready(swap(chunks[1] + part[size:], "src", MASKS[1]))


def target_totals(waves, between):
    first = reduce(waves[0], REDUCE_STEPWISE[0], lambda parts: parts)
    made = between(first)
    second = reduce(waves[1], REDUCE_STEPWISE[1], lambda parts: tie(parts, made))
    sums = [first, second]
    for mask in higher_masks("src", GROUP):
        parts = [swap(value, "src", mask) for value in sums]
        parts[0] = tie(parts[0], sums[1])
        sums = [value + part for value, part in zip(sums, parts)]
    return [chunk for value, stepwise in zip(sums, SPREAD_STEPWISE) for chunk in spread(value, stepwise)], made


def source_totals(pieces):
    own = [mine + swap(theirs, "tgt", 1) for mine, theirs in zip(pieces[:PIECES], pieces[PIECES:])]
    for mask in higher_masks("tgt", 2):
        own = [value + swap(value, "tgt", mask) for value in own]
    return own + [swap(value, "tgt", 1) for value in own]


def body(
    edge_state,
    edge_source,
    edge_target,
    live_edges,
    inner_one,
    outer_one,
    inner_two,
    outer_two,
    gain_one,
    gain_two,
):
    rows, channels = edge_state.shape[2:]
    states = edge_state.reshape(rows, channels)
    sources = edge_source.reshape(1, rows)
    targets = edge_target.reshape(1, rows)
    target_atoms = ATOM_DEV * lax.axis_size("src")
    source_atoms = ATOM_DEV * lax.axis_size("tgt")
    sizes = wave_sizes(target_atoms)
    half = source_atoms // 2
    first, live, targets, states = first_sums(states, targets, live_edges, sizes)
    waves = [first] + [later_sums(states, targets, live, wave, sizes) for wave in range(1, len(sizes))]

    def choose(first):
        return call(
            functools.partial(choose_kernel, sizes, half),
            [
                jax.ShapeDtypeStruct((rows, target_atoms), jnp.bfloat16),
                jax.ShapeDtypeStruct((rows, source_atoms), jnp.bfloat16),
                jax.ShapeDtypeStruct((source_atoms, rows), jnp.bfloat16),
            ],
            [VMEM] * 3, HIDE_FLOPS,
        )(targets, sources, first)

    totals, (target_chosen, source_chosen, source_pick) = target_totals(waves, choose)
    reverse_state, *pieces = call(
        functools.partial(layer_one_kernel, len(totals)),
        [jax.ShapeDtypeStruct((rows, channels), jnp.bfloat16)]
        + [jax.ShapeDtypeStruct((half // PIECES, channels), jnp.float32)] * (2 * PIECES),
        [VMEM] * (len(totals) + 7),
        2 * rows * channels * (3 * target_atoms + 2 * channels + source_atoms),
        [pltpu.VMEM((3 * target_atoms, channels), jnp.bfloat16)],
    )(live, *totals, target_chosen, source_pick, states, inner_one, outer_one, gain_one.reshape(1, channels))
    totals = source_totals(pieces)
    final_state = call(
        functools.partial(layer_two_kernel, len(totals)),
        jax.ShapeDtypeStruct((rows, channels), jnp.bfloat16),
        [VMEM] * (len(totals) + 6),
        2 * rows * channels * (3 * source_atoms + 2 * channels),
        [
            pltpu.VMEM((3 * source_atoms, channels), jnp.bfloat16),
            pltpu.VMEM((rows, channels), jnp.bfloat16),
            pltpu.SemaphoreType.DMA((2,)),
        ],
        HBM,
    )(live, *totals, source_chosen, reverse_state, inner_two, outer_two, gain_two.reshape(1, channels))
    return final_state.reshape(1, 1, rows, channels)


def solution(mesh):
    placed = (
        P("src", "tgt", None, None),
        P("src", "tgt", None),
        P("src", "tgt", None),
        P("src", "tgt"),
        P(),
        P(),
        P(),
        P(),
        P(),
        P(),
    )
    return jax.shard_map(
        body, mesh=mesh, in_specs=placed, out_specs=P("src", "tgt", None, None), check_vma=False
    )
```

```python
import functools

import jax
import jax.numpy as jnp
from jax import lax
from jax.experimental import pallas as pl
from jax.experimental.pallas import tpu as pltpu
from jax.sharding import PartitionSpec as P

ATOM_DEV = 64
GROUP = 4
NEAR, FAR, BOTH = 1, 2, 3
SHARES = (4, 4)
REDUCE_STEPWISE = (False, True)
SPREAD_STEPWISE = (False, False)
PIECES = 2
PARTS = 2
LANES = 128
HIDE_FLOPS = 8 * 10**9
VMEM_LIMIT = 40 * 1024 * 1024
FIRST_VMEM_LIMIT = 52 * 1024 * 1024

VMEM = pl.BlockSpec(memory_space=pltpu.VMEM)
HBM = pl.BlockSpec(memory_space=pltpu.HBM)


def call(kernel, out_shape, in_specs, flops, scratch=(), out_specs=None, limit=VMEM_LIMIT):
    return pl.pallas_call(
        kernel,
        out_shape=out_shape,
        in_specs=in_specs,
        out_specs=jax.tree.map(lambda _: VMEM, out_shape) if out_specs is None else out_specs,
        scratch_shapes=list(scratch),
        compiler_params=pltpu.CompilerParams(vmem_limit_bytes=limit),
        cost_estimate=pl.CostEstimate(flops=flops, bytes_accessed=0, transcendentals=0),
    )


def wave_sizes(atoms):
    return [atoms // (GROUP * sum(SHARES)) * share for share in SHARES]


def partner_mask(kind, core):
    if kind in (NEAR, FAR) and core == 0:
        return NEAR + FAR - kind
    return kind


def target_place(atoms, sizes):
    device = lax.axis_index("src")
    low, high = device % 2, (device // 2) % 2
    own = jnp.where(lax.axis_index("tgt") % 2 == 0, high + 2 * low, low + 2 * high)
    place = atoms
    base = 0
    for size in sizes:
        inside = atoms - base
        chunk = sum((inside >= k * size).astype(jnp.int32) for k in range(1, GROUP))
        spot = base + jnp.bitwise_xor(chunk, own) * size + inside - chunk * size
        place = jnp.where(inside >= 0, spot, place)
        base += GROUP * size
    return place


def source_place(atoms, half):
    return jnp.bitwise_xor(atoms, (lax.axis_index("tgt") % 2) * half)


def one_hot(place, slot):
    return jnp.where(place == slot, jnp.float32(1.0), jnp.float32(0.0)).astype(jnp.bfloat16)


def store_sums(wave, sizes, live, targets, fetch, chunk_refs):
    rows = targets.shape[1]
    size = sizes[wave]
    place = target_place(targets, sizes)
    place = jnp.where(lax.broadcasted_iota(jnp.int32, (1, rows), 1) < live, place, -1)
    slot = lax.broadcasted_iota(jnp.int32, (size * GROUP, rows), 0) + sum(sizes[:wave]) * GROUP
    chosen = one_hot(place, slot)
    total = fetch(chosen)
    at = 0
    for chunk_ref in chunk_refs:
        count = chunk_ref.shape[0]
        chunk_ref[...] = total[at : at + count]
        at += count


def first_sum_kernel(sizes, live_hbm, target_hbm, state_hbm, *refs):
    *chunk_refs, live_out, target_ref, state_ref, live_ref, sems = refs
    rows = state_ref.shape[0]
    blocks = [pl.ds(first, rows // PARTS) for first in range(0, rows, rows // PARTS)]
    copies = [
        pltpu.make_async_copy(source, place, sems.at[index])
        for index, (source, place) in enumerate(
            [(live_hbm, live_ref), (target_hbm, target_ref)]
            + [(state_hbm.at[block], state_ref.at[block]) for block in blocks]
        )
    ]
    for copy in copies:
        copy.start()
    copies[0].wait()
    live = live_ref[0, 0]
    live_out[...] = jnp.full(live_out.shape, live, jnp.int32)
    copies[1].wait()

    def fetch(chosen):
        total = None
        for index, block in enumerate(blocks):
            copies[2 + index].wait()
            part = slice(index * block.size, (index + 1) * block.size)
            term = jnp.dot(chosen[:, part], state_ref[block, :], preferred_element_type=jnp.float32)
            total = term if total is None else total + term
        return total

    store_sums(0, sizes, live, target_ref[...], fetch, chunk_refs)


def later_sum_kernel(wave, sizes, live_ref, target_ref, state_ref, *chunk_refs):
    store_sums(wave, sizes, live_ref[:, :1], target_ref[...], lambda chosen: jnp.dot(chosen, state_ref[...], preferred_element_type=jnp.float32), chunk_refs)


def chunk_shapes(wave, size, channels):
    counts = [size, size, 2 * size] if REDUCE_STEPWISE[wave] else [size] * GROUP
    return [jax.ShapeDtypeStruct((count, channels), jnp.float32) for count in counts]


def first_sums(states, targets, live, sizes):
    rows, channels = states.shape
    handed_on = [
        jax.ShapeDtypeStruct((1, LANES), jnp.int32),
        jax.ShapeDtypeStruct(targets.shape, targets.dtype),
        jax.ShapeDtypeStruct(states.shape, states.dtype),
    ]
    out = call(
        functools.partial(first_sum_kernel, sizes), chunk_shapes(0, sizes[0], channels) + handed_on, [HBM] * 3,
        2 * sizes[0] * GROUP * rows * channels,
        [pltpu.SMEM((1, 1), jnp.int32), pltpu.SemaphoreType.DMA((2 + PARTS,))],
        limit=FIRST_VMEM_LIMIT,
    )(live, targets, states)
    return out[:-3], *out[-3:]


def later_sums(states, targets, live, wave, sizes):
    rows, channels = states.shape
    return call(
        functools.partial(later_sum_kernel, wave, sizes), chunk_shapes(wave, sizes[wave], channels), [VMEM] * 3,
        2 * sizes[wave] * GROUP * rows * channels,
    )(live, targets, states)


def choose_kernel(sizes, half, target_ref, source_ref, tie_ref, target_chosen_ref, source_chosen_ref, source_pick_ref):
    del tie_ref
    rows = target_ref.shape[1]
    sources = source_place(source_ref[...], half)
    for values, chosen_ref in ((target_place(target_ref[...], sizes), target_chosen_ref), (sources, source_chosen_ref)):
        place = jnp.transpose(jnp.broadcast_to(values, (LANES, rows)))
        lane = lax.broadcasted_iota(jnp.int32, (rows, LANES), 1)
        for first in range(0, chosen_ref.shape[1], LANES):
            chosen_ref[:, first : first + LANES] = one_hot(place, lane + first)
    source_pick_ref[...] = one_hot(sources, lax.broadcasted_iota(jnp.int32, source_pick_ref.shape, 0))


def split_sums(sum_refs, parts_ref):
    total = parts_ref.shape[0] // 3
    at = 0
    for sum_ref in sum_refs:
        size = sum_ref.shape[0]
        value = sum_ref[...]
        for part in range(3):
            low = value.astype(jnp.bfloat16)
            parts_ref[part * total + at : part * total + at + size, :] = low
            value = value - low.astype(jnp.float32)
        at += size


def normed_activated(chosen_ref, parts_ref, state_ref, inner_ref, gain_ref):
    chosen = chosen_ref[...]
    gathered = jnp.dot(
        jnp.concatenate([chosen, chosen, chosen], axis=1), parts_ref[...], preferred_element_type=jnp.float32
    )
    message = gathered - state_ref[...].astype(jnp.float32)
    mean_square = jnp.mean(message * message, axis=-1, keepdims=True)
    normed = message * lax.rsqrt(mean_square + 1e-05) * gain_ref[...]
    activated = jax.nn.relu(
        jnp.dot(normed.astype(jnp.bfloat16), inner_ref[...], preferred_element_type=jnp.float32)
    ).astype(jnp.bfloat16)
    return normed, activated


def finish(normed, activated, outer_ref, live_ref, first_row):
    result = normed + jnp.dot(activated, outer_ref[...], preferred_element_type=jnp.float32)
    row = lax.broadcasted_iota(jnp.int32, (result.shape[0], 1), 0) + first_row
    return jnp.where(row < live_ref[:, :1], result, jnp.float32(0.0)).astype(jnp.bfloat16)


def layer_one_kernel(n_sums, live_ref, *refs):
    sum_refs = refs[:n_sums]
    chosen_ref, pick_ref, state_ref, inner_ref, outer_ref, gain_ref, reverse_ref, *piece_refs, parts_ref = refs[n_sums:]
    split_sums(sum_refs, parts_ref)
    normed, activated = normed_activated(chosen_ref, parts_ref, state_ref, inner_ref, gain_ref)
    reverse_ref[...] = finish(normed, activated, outer_ref, live_ref, 0)
    total = jnp.dot(pick_ref[...], reverse_ref[...], preferred_element_type=jnp.float32)
    size = piece_refs[0].shape[0]
    for index, piece_ref in enumerate(piece_refs):
        piece_ref[...] = total[index * size : (index + 1) * size]


def layer_two_kernel(n_sums, live_ref, *refs):
    sum_refs = refs[:n_sums]
    chosen_ref, state_ref, inner_ref, outer_ref, gain_ref, final_hbm, parts_ref, final_ref, sems = refs[n_sums:]
    split_sums(sum_refs, parts_ref)
    normed, activated = normed_activated(chosen_ref, parts_ref, state_ref, inner_ref, gain_ref)
    block = final_ref.shape[0] // 2
    copies = []
    for index in range(2):
        rows = pl.ds(index * block, block)
        part = slice(index * block, (index + 1) * block)
        final_ref[rows, :] = finish(normed[part], activated[part], outer_ref, live_ref, index * block)
        copies.append(pltpu.make_async_copy(final_ref.at[rows], final_hbm.at[rows], sems.at[index]))
        copies[-1].start()
    for copy in copies:
        copy.wait()


def swap(value, axis, mask):
    return lax.ppermute(value, axis, [(i, i ^ mask) for i in range(lax.axis_size(axis))])


def swap_group(value, kind):
    across = lax.axis_size("tgt")
    return lax.ppermute(
        value,
        ("src", "tgt"),
        [
            (i * across + j, (i ^ partner_mask(kind, j % 2)) * across + j)
            for i in range(lax.axis_size("src"))
            for j in range(across)
        ],
    )


def higher_masks(axis, low):
    masks = []
    while low < lax.axis_size(axis):
        masks.append(low)
        low *= 2
    return masks


def tie(value, other):
    return lax.optimization_barrier((value, other))[0]


def spread(total, stepwise):
    if not stepwise:
        return [total] + [swap_group(total, kind) for kind in (NEAR, FAR, BOTH)]
    near = swap_group(total, NEAR)
    return [total, near, swap_group(jnp.concatenate([total, near]), FAR)]


def reduce(chunks, stepwise, ready):
    if not stepwise:
        parts = ready([swap_group(chunks[kind], kind) for kind in (BOTH, NEAR, FAR)])
        return chunks[0] + parts[0] + parts[1] + parts[2]
    size = chunks[0].shape[0]
    part = swap_group(chunks[2], FAR)
    return chunks[0] + part[:size] + ready(swap_group(chunks[1] + part[size:], NEAR))


def target_totals(waves, between):
    first = reduce(waves[0], REDUCE_STEPWISE[0], lambda parts: parts)
    made = between(first)
    second = reduce(waves[1], REDUCE_STEPWISE[1], lambda parts: tie(parts, made))
    sums = [first, second]
    for mask in higher_masks("src", GROUP):
        parts = [swap(value, "src", mask) for value in sums]
        sums = [value + part for value, part in zip(sums, parts)]
    return [chunk for value, stepwise in zip(sums, SPREAD_STEPWISE) for chunk in spread(value, stepwise)], made


def source_totals(pieces):
    own = [mine + swap(theirs, "tgt", 1) for mine, theirs in zip(pieces[:PIECES], pieces[PIECES:])]
    for mask in higher_masks("tgt", 2):
        own = [value + swap(value, "tgt", mask) for value in own]
    return own + [swap(value, "tgt", 1) for value in own]


def body(
    edge_state,
    edge_source,
    edge_target,
    live_edges,
    inner_one,
    outer_one,
    inner_two,
    outer_two,
    gain_one,
    gain_two,
):
    rows, channels = edge_state.shape[2:]
    states = edge_state.reshape(rows, channels)
    sources = edge_source.reshape(1, rows)
    targets = edge_target.reshape(1, rows)
    target_atoms = ATOM_DEV * lax.axis_size("src")
    source_atoms = ATOM_DEV * lax.axis_size("tgt")
    sizes = wave_sizes(target_atoms)
    half = source_atoms // 2
    first, live, targets, states = first_sums(states, targets, live_edges, sizes)
    waves = [first] + [later_sums(states, targets, live, wave, sizes) for wave in range(1, len(sizes))]

    def choose(first):
        return call(
            functools.partial(choose_kernel, sizes, half),
            [
                jax.ShapeDtypeStruct((rows, target_atoms), jnp.bfloat16),
                jax.ShapeDtypeStruct((rows, source_atoms), jnp.bfloat16),
                jax.ShapeDtypeStruct((source_atoms, rows), jnp.bfloat16),
            ],
            [VMEM] * 3, HIDE_FLOPS,
        )(targets, sources, first)

    totals, (target_chosen, source_chosen, source_pick) = target_totals(waves, choose)
    reverse_state, *pieces = call(
        functools.partial(layer_one_kernel, len(totals)),
        [jax.ShapeDtypeStruct((rows, channels), jnp.bfloat16)]
        + [jax.ShapeDtypeStruct((half // PIECES, channels), jnp.float32)] * (2 * PIECES),
        [VMEM] * (len(totals) + 7),
        2 * rows * channels * (3 * target_atoms + 2 * channels + source_atoms),
        [pltpu.VMEM((3 * target_atoms, channels), jnp.bfloat16)],
    )(live, *totals, target_chosen, source_pick, states, inner_one, outer_one, gain_one.reshape(1, channels))
    totals = source_totals(pieces)
    final_state = call(
        functools.partial(layer_two_kernel, len(totals)),
        jax.ShapeDtypeStruct((rows, channels), jnp.bfloat16),
        [VMEM] * (len(totals) + 6),
        2 * rows * channels * (3 * source_atoms + 2 * channels),
        [
            pltpu.VMEM((3 * source_atoms, channels), jnp.bfloat16),
            pltpu.VMEM((rows, channels), jnp.bfloat16),
            pltpu.SemaphoreType.DMA((2,)),
        ],
        HBM,
    )(live, *totals, source_chosen, reverse_state, inner_two, outer_two, gain_two.reshape(1, channels))
    return final_state.reshape(1, 1, rows, channels)


def solution(mesh):
    placed = (
        P("src", "tgt", None, None),
        P("src", "tgt", None),
        P("src", "tgt", None),
        P("src", "tgt"),
        P(),
        P(),
        P(),
        P(),
        P(),
        P(),
    )
    return jax.shard_map(
        body, mesh=mesh, in_specs=placed, out_specs=P("src", "tgt", None, None), check_vma=False
    )
```

```python
import functools

import jax
import jax.numpy as jnp
from jax import lax
from jax.experimental import pallas as pl
from jax.experimental.pallas import tpu as pltpu
from jax.sharding import PartitionSpec as P

ATOM_DEV = 64
GROUP = 4
NEAR, FAR, BOTH = 1, 2, 3
SHARES = (4, 4)
REDUCE_STEPWISE = (False, True)
SPREAD_STEPWISE = (False, False)
PIECES = (1, 1)
PARTS = 2
LANES = 128
HIDE_FLOPS = 8 * 10**9
VMEM_LIMIT = 40 * 1024 * 1024

VMEM = pl.BlockSpec(memory_space=pltpu.VMEM)
HBM = pl.BlockSpec(memory_space=pltpu.HBM)
SMEM = pl.BlockSpec(memory_space=pltpu.SMEM)


def call(kernel, out_shape, in_specs, flops, scratch=(), out_specs=None):
    return pl.pallas_call(
        kernel,
        out_shape=out_shape,
        in_specs=in_specs,
        out_specs=jax.tree.map(lambda _: VMEM, out_shape) if out_specs is None else out_specs,
        scratch_shapes=list(scratch),
        compiler_params=pltpu.CompilerParams(vmem_limit_bytes=VMEM_LIMIT),
        cost_estimate=pl.CostEstimate(flops=flops, bytes_accessed=0, transcendentals=0),
    )


def wave_sizes(atoms):
    return [atoms // (GROUP * sum(SHARES)) * share for share in SHARES]


def partner_mask(kind, core):
    if kind in (NEAR, FAR) and core == 0:
        return NEAR + FAR - kind
    return kind


def target_place(atoms, sizes):
    device = lax.axis_index("src")
    low, high = device % 2, (device // 2) % 2
    own = jnp.where(lax.axis_index("tgt") % 2 == 0, high + 2 * low, low + 2 * high)
    place = atoms
    base = 0
    for size in sizes:
        inside = atoms - base
        chunk = sum((inside >= k * size).astype(jnp.int32) for k in range(1, GROUP))
        spot = base + jnp.bitwise_xor(chunk, own) * size + inside - chunk * size
        place = jnp.where(inside >= 0, spot, place)
        base += GROUP * size
    return place


def piece_sizes(half):
    return [half // sum(PIECES) * piece for piece in PIECES]


def source_place(atoms, half):
    own = (lax.axis_index("tgt") % 2) * half
    ours = jnp.bitwise_xor(atoms, own)
    other = (ours >= half).astype(jnp.int32)
    inside = ours - other * half
    place = atoms
    base = 0
    for size in piece_sizes(half):
        place = jnp.where(inside >= base, 2 * base + other * size + inside - base, place)
        base += size
    return place


def one_hot(place, slot):
    return jnp.where(place == slot, jnp.float32(1.0), jnp.float32(0.0)).astype(jnp.bfloat16)


def store_sums(wave, sizes, live, targets, fetch, chunk_refs):
    rows = targets.shape[1]
    size = sizes[wave]
    place = target_place(targets, sizes)
    place = jnp.where(lax.broadcasted_iota(jnp.int32, (1, rows), 1) < live, place, -1)
    slot = lax.broadcasted_iota(jnp.int32, (size * GROUP, rows), 0) + sum(sizes[:wave]) * GROUP
    chosen = one_hot(place, slot)
    total = fetch(chosen)
    at = 0
    for chunk_ref in chunk_refs:
        count = chunk_ref.shape[0]
        chunk_ref[...] = total[at : at + count]
        at += count


def first_sum_kernel(sizes, live_ref, target_hbm, state_hbm, *refs):
    *chunk_refs, live_out, target_ref, state_ref, sems = refs
    rows = state_ref.shape[0]
    blocks = [pl.ds(first, rows // PARTS) for first in range(0, rows, rows // PARTS)]
    copies = [
        pltpu.make_async_copy(source, place, sems.at[index])
        for index, (source, place) in enumerate(
            [(target_hbm, target_ref)] + [(state_hbm.at[block], state_ref.at[block]) for block in blocks]
        )
    ]
    for copy in copies:
        copy.start()
    live = live_ref[0, 0]
    live_out[...] = jnp.full(live_out.shape, live, jnp.int32)
    copies[0].wait()

    def fetch(chosen):
        total = None
        for index, block in enumerate(blocks):
            copies[1 + index].wait()
            part = slice(index * block.size, (index + 1) * block.size)
            term = jnp.dot(chosen[:, part], state_ref[block, :], preferred_element_type=jnp.float32)
            total = term if total is None else total + term
        return total

    store_sums(0, sizes, live, target_ref[...], fetch, chunk_refs)


def later_sum_kernel(wave, sizes, live_ref, target_ref, state_ref, *chunk_refs):
    def fetch(chosen):
        return jnp.dot(chosen, state_ref[...], preferred_element_type=jnp.float32)

    store_sums(wave, sizes, live_ref[:, :1], target_ref[...], fetch, chunk_refs)


def chunk_shapes(wave, size, channels):
    counts = [size, size, 2 * size] if REDUCE_STEPWISE[wave] else [size] * GROUP
    return [jax.ShapeDtypeStruct((count, channels), jnp.float32) for count in counts]


def first_sums(states, targets, live, sizes):
    rows, channels = states.shape
    handed_on = [
        jax.ShapeDtypeStruct((1, LANES), jnp.int32),
        jax.ShapeDtypeStruct(targets.shape, targets.dtype),
        jax.ShapeDtypeStruct(states.shape, states.dtype),
    ]
    out = call(
        functools.partial(first_sum_kernel, sizes), chunk_shapes(0, sizes[0], channels) + handed_on, [SMEM, HBM, HBM],
        2 * sizes[0] * GROUP * rows * channels,
        [pltpu.SemaphoreType.DMA((1 + PARTS,))],
    )(live, *(pltpu.with_memory_space_constraint(value, pltpu.HBM) for value in (targets, states)))
    return out[:-3], *out[-3:]


def later_sums(states, targets, live, wave, sizes):
    rows, channels = states.shape
    return call(
        functools.partial(later_sum_kernel, wave, sizes), chunk_shapes(wave, sizes[wave], channels), [VMEM] * 3,
        2 * sizes[wave] * GROUP * rows * channels,
    )(live, targets, states)


def choose_kernel(sizes, half, target_ref, source_ref, tie_ref, *refs):
    del tie_ref
    rows = target_ref.shape[1]
    sources = source_place(source_ref[...], half)
    pick_ref, refs = refs[0], refs[1:]
    for place, part_refs in ((target_place(target_ref[...], sizes), refs[: len(sizes)]), (sources, refs[len(sizes) :])):
        place = jnp.transpose(jnp.broadcast_to(place, (LANES, rows)))
        base = 0
        for part_ref in part_refs:
            count = part_ref.shape[1]
            for first in range(0, count, LANES):
                width = min(LANES, count - first)
                lane = lax.broadcasted_iota(jnp.int32, (rows, width), 1) + (base + first)
                part_ref[:, first : first + width] = one_hot(place[:, :width], lane)
            base += count
    pick_ref[...] = one_hot(sources, lax.broadcasted_iota(jnp.int32, pick_ref.shape, 0))


def split_sums(sum_refs, parts_ref):
    total = parts_ref.shape[0] // 3
    at = 0
    for sum_ref in sum_refs:
        size = sum_ref.shape[0]
        value = sum_ref[...]
        for part in range(3):
            low = value.astype(jnp.bfloat16)
            parts_ref[part * total + at : part * total + at + size, :] = low
            value = value - low.astype(jnp.float32)
        at += size


def gather(chosen_ref, parts_ref):
    chosen = chosen_ref[...]
    return jnp.dot(
        jnp.concatenate([chosen, chosen, chosen], axis=1), parts_ref[...], preferred_element_type=jnp.float32
    )


def gather_kernel(n_sums, *refs):
    sum_refs = refs[:n_sums]
    chosen_ref, gathered_ref, parts_ref = refs[n_sums:]
    split_sums(sum_refs, parts_ref)
    gathered_ref[...] = gather(chosen_ref, parts_ref)


def gather_first(sums, chosen):
    rows, count = chosen.shape
    channels = sums[0].shape[1]
    return call(
        functools.partial(gather_kernel, len(sums)),
        jax.ShapeDtypeStruct((rows, channels), jnp.float32),
        [VMEM] * (len(sums) + 1), 6 * rows * count * channels,
        [pltpu.VMEM((3 * count, channels), jnp.bfloat16)],
    )(*sums, chosen)


def normed_activated(gathered_ref, chosen_ref, parts_ref, state_ref, inner_ref, gain_ref):
    message = gathered_ref[...] + gather(chosen_ref, parts_ref) - state_ref[...].astype(jnp.float32)
    mean_square = jnp.mean(message * message, axis=-1, keepdims=True)
    normed = message * lax.rsqrt(mean_square + 1e-05) * gain_ref[...]
    activated = jax.nn.relu(
        jnp.dot(normed.astype(jnp.bfloat16), inner_ref[...], preferred_element_type=jnp.float32)
    ).astype(jnp.bfloat16)
    return normed, activated


def finish(normed, activated, outer_ref, live_ref, first_row):
    result = normed + jnp.dot(activated, outer_ref[...], preferred_element_type=jnp.float32)
    row = lax.broadcasted_iota(jnp.int32, (result.shape[0], 1), 0) + first_row
    return jnp.where(row < live_ref[:, :1], result, jnp.float32(0.0)).astype(jnp.bfloat16)


def layer_one_kernel(n_sums, live_ref, *refs):
    sum_refs = refs[:n_sums]
    gathered_ref, chosen_ref, pick_ref, state_ref, inner_ref, outer_ref, gain_ref, reverse_ref, *piece_refs, parts_ref = refs[n_sums:]
    split_sums(sum_refs, parts_ref)
    normed, activated = normed_activated(gathered_ref, chosen_ref, parts_ref, state_ref, inner_ref, gain_ref)
    reverse_ref[...] = finish(normed, activated, outer_ref, live_ref, 0)
    total = jnp.dot(pick_ref[...], reverse_ref[...], preferred_element_type=jnp.float32)
    at = 0
    for piece_ref in piece_refs:
        count = piece_ref.shape[0]
        piece_ref[...] = total[at : at + count]
        at += count


def layer_two_kernel(n_sums, live_ref, *refs):
    sum_refs = refs[:n_sums]
    gathered_ref, chosen_ref, state_ref, inner_ref, outer_ref, gain_ref, final_hbm, parts_ref, final_ref, sems = refs[n_sums:]
    split_sums(sum_refs, parts_ref)
    normed, activated = normed_activated(gathered_ref, chosen_ref, parts_ref, state_ref, inner_ref, gain_ref)
    block = final_ref.shape[0] // 2
    copies = []
    for index in range(2):
        rows = pl.ds(index * block, block)
        part = slice(index * block, (index + 1) * block)
        final_ref[rows, :] = finish(normed[part], activated[part], outer_ref, live_ref, index * block)
        copies.append(pltpu.make_async_copy(final_ref.at[rows], final_hbm.at[rows], sems.at[index]))
        copies[-1].start()
    for copy in copies:
        copy.wait()


def swap(value, axis, mask):
    return lax.ppermute(value, axis, [(i, i ^ mask) for i in range(lax.axis_size(axis))])


def swap_group(value, kind):
    across = lax.axis_size("tgt")
    return lax.ppermute(
        value,
        ("src", "tgt"),
        [
            (i * across + j, (i ^ partner_mask(kind, j % 2)) * across + j)
            for i in range(lax.axis_size("src"))
            for j in range(across)
        ],
    )


def higher_masks(axis, low):
    masks = []
    while low < lax.axis_size(axis):
        masks.append(low)
        low *= 2
    return masks


def tie(value, other):
    return lax.optimization_barrier((value, other))[0]


def spread(total, stepwise):
    if not stepwise:
        return [total] + [swap_group(total, kind) for kind in (NEAR, FAR, BOTH)]
    near = swap_group(total, NEAR)
    return [total, near, swap_group(jnp.concatenate([total, near]), FAR)]


def reduce(chunks, stepwise, ready):
    if not stepwise:
        parts = ready([swap_group(chunks[kind], kind) for kind in (BOTH, NEAR, FAR)])
        return chunks[0] + parts[0] + parts[1] + parts[2]
    size = chunks[0].shape[0]
    part = swap_group(chunks[2], FAR)
    return chunks[0] + part[:size] + ready(swap_group(chunks[1] + part[size:], NEAR))


def target_totals(waves, between):
    first = reduce(waves[0], REDUCE_STEPWISE[0], lambda parts: parts)
    made = between(first)
    second = reduce(waves[1], REDUCE_STEPWISE[1], lambda parts: tie(parts, made))
    sums = [first, second]
    for mask in higher_masks("src", GROUP):
        parts = [swap(value, "src", mask) for value in sums]
        sums = [value + part for value, part in zip(sums, parts)]
    return [spread(value, stepwise) for value, stepwise in zip(sums, SPREAD_STEPWISE)], made


def source_totals(pieces):
    own = [mine + swap(theirs, "tgt", 1) for mine, theirs in pieces]
    for mask in higher_masks("tgt", 2):
        own = [value + swap(value, "tgt", mask) for value in own]
    return [[value, swap(value, "tgt", 1)] for value in own]


def body(
    edge_state,
    edge_source,
    edge_target,
    live_edges,
    inner_one,
    outer_one,
    inner_two,
    outer_two,
    gain_one,
    gain_two,
):
    rows, channels = edge_state.shape[2:]
    states = edge_state.reshape(rows, channels)
    sources = edge_source.reshape(1, rows)
    targets = edge_target.reshape(1, rows)
    target_atoms = ATOM_DEV * lax.axis_size("src")
    source_atoms = ATOM_DEV * lax.axis_size("tgt")
    sizes = wave_sizes(target_atoms)
    half = source_atoms // 2
    first, live, targets, states = first_sums(states, targets, live_edges, sizes)
    waves = [first] + [later_sums(states, targets, live, wave, sizes) for wave in range(1, len(sizes))]

    pieces = piece_sizes(half)
    n_waves = len(sizes)

    def choose(first):
        return call(
            functools.partial(choose_kernel, sizes, half),
            [jax.ShapeDtypeStruct((source_atoms, rows), jnp.bfloat16)]
            + [jax.ShapeDtypeStruct((rows, GROUP * size), jnp.bfloat16) for size in sizes]
            + [jax.ShapeDtypeStruct((rows, 2 * size), jnp.bfloat16) for size in pieces],
            [VMEM] * 3, HIDE_FLOPS,
        )(targets, sources, first)

    totals, (source_pick, *chosen) = target_totals(waves, choose)
    target_chosen, source_chosen = chosen[:n_waves], chosen[n_waves:]
    gathered = gather_first(totals[0], target_chosen[0])
    reverse_state, *sums = call(
        functools.partial(layer_one_kernel, len(totals[1])),
        [jax.ShapeDtypeStruct((rows, channels), jnp.bfloat16)]
        + [jax.ShapeDtypeStruct((size, channels), jnp.float32) for size in pieces for _ in range(2)],
        [VMEM] * (len(totals[1]) + 8),
        2 * rows * channels * (3 * GROUP * sizes[1] + 2 * channels + source_atoms),
        [pltpu.VMEM((3 * GROUP * sizes[1], channels), jnp.bfloat16)],
    )(live, *totals[1], gathered, target_chosen[1], source_pick, states, inner_one, outer_one, gain_one.reshape(1, channels))
    totals = source_totals(list(zip(sums[::2], sums[1::2])))
    gathered = gather_first(totals[0], source_chosen[0])
    final_state = call(
        functools.partial(layer_two_kernel, len(totals[1])),
        jax.ShapeDtypeStruct((rows, channels), jnp.bfloat16),
        [VMEM] * (len(totals[1]) + 7),
        2 * rows * channels * (6 * pieces[1] + 2 * channels),
        [
            pltpu.VMEM((6 * pieces[1], channels), jnp.bfloat16),
            pltpu.VMEM((rows, channels), jnp.bfloat16),
            pltpu.SemaphoreType.DMA((2,)),
        ],
        HBM,
    )(live, *totals[1], gathered, source_chosen[1], reverse_state, inner_two, outer_two, gain_two.reshape(1, channels))
    return final_state.reshape(1, 1, rows, channels)


def solution(mesh):
    placed = (
        P("src", "tgt", None, None),
        P("src", "tgt", None),
        P("src", "tgt", None),
        P("src", "tgt"),
        P(),
        P(),
        P(),
        P(),
        P(),
        P(),
    )
    return jax.shard_map(
        body, mesh=mesh, in_specs=placed, out_specs=P("src", "tgt", None, None), check_vma=False
    )
```

```python
import functools

import jax
import jax.numpy as jnp
from jax import lax
from jax.experimental import pallas as pl
from jax.experimental.pallas import tpu as pltpu
from jax.sharding import PartitionSpec as P

ATOM_DEV = 64
GROUP = 4
NEAR, FAR, BOTH = 1, 2, 3
SHARES = (4, 4)
REDUCE_STEPWISE = (False, True)
SPREAD_STEPWISE = (False, False)
PIECES = (1, 1)
PARTS = 2
LANES = 128
HIDE_FLOPS = 8 * 10**9
VMEM_LIMIT = 40 * 1024 * 1024

VMEM = pl.BlockSpec(memory_space=pltpu.VMEM)
HBM = pl.BlockSpec(memory_space=pltpu.HBM)
SMEM = pl.BlockSpec(memory_space=pltpu.SMEM)


def call(kernel, out_shape, in_specs, flops, scratch=(), out_specs=None):
    return pl.pallas_call(
        kernel,
        out_shape=out_shape,
        in_specs=in_specs,
        out_specs=jax.tree.map(lambda _: VMEM, out_shape) if out_specs is None else out_specs,
        scratch_shapes=list(scratch),
        compiler_params=pltpu.CompilerParams(vmem_limit_bytes=VMEM_LIMIT),
        cost_estimate=pl.CostEstimate(flops=flops, bytes_accessed=0, transcendentals=0),
    )


def wave_sizes(atoms):
    return [atoms // (GROUP * sum(SHARES)) * share for share in SHARES]


def partner_mask(kind, core):
    if kind in (NEAR, FAR) and core == 0:
        return NEAR + FAR - kind
    return kind


def target_place(atoms, sizes):
    device = lax.axis_index("src")
    low, high = device % 2, (device // 2) % 2
    own = jnp.where(lax.axis_index("tgt") % 2 == 0, high + 2 * low, low + 2 * high)
    place = atoms
    base = 0
    for size in sizes:
        inside = atoms - base
        chunk = sum((inside >= k * size).astype(jnp.int32) for k in range(1, GROUP))
        spot = base + jnp.bitwise_xor(chunk, own) * size + inside - chunk * size
        place = jnp.where(inside >= 0, spot, place)
        base += GROUP * size
    return place


def piece_sizes(half):
    return [half // sum(PIECES) * piece for piece in PIECES]


def source_place(atoms, half):
    own = (lax.axis_index("tgt") % 2) * half
    ours = jnp.bitwise_xor(atoms, own)
    other = (ours >= half).astype(jnp.int32)
    inside = ours - other * half
    place = atoms
    base = 0
    for size in piece_sizes(half):
        place = jnp.where(inside >= base, 2 * base + other * size + inside - base, place)
        base += size
    return place


def one_hot(place, slot):
    return jnp.where(place == slot, jnp.float32(1.0), jnp.float32(0.0)).astype(jnp.bfloat16)


def store_sums(wave, sizes, live, targets, fetch, chunk_refs):
    rows = targets.shape[1]
    size = sizes[wave]
    place = target_place(targets, sizes)
    place = jnp.where(lax.broadcasted_iota(jnp.int32, (1, rows), 1) < live, place, -1)
    slot = lax.broadcasted_iota(jnp.int32, (size * GROUP, rows), 0) + sum(sizes[:wave]) * GROUP
    chosen = one_hot(place, slot)
    total = fetch(chosen)
    at = 0
    for chunk_ref in chunk_refs:
        count = chunk_ref.shape[0]
        chunk_ref[...] = total[at : at + count]
        at += count


def first_sum_kernel(sizes, live_ref, target_hbm, state_hbm, *refs):
    *chunk_refs, live_out, target_ref, state_ref, sems = refs
    rows = state_ref.shape[0]
    blocks = [pl.ds(first, rows // PARTS) for first in range(0, rows, rows // PARTS)]
    copies = [
        pltpu.make_async_copy(source, place, sems.at[index])
        for index, (source, place) in enumerate(
            [(target_hbm, target_ref)] + [(state_hbm.at[block], state_ref.at[block]) for block in blocks]
        )
    ]
    for copy in copies:
        copy.start()
    live = live_ref[0, 0]
    live_out[...] = jnp.full(live_out.shape, live, jnp.int32)
    copies[0].wait()

    def fetch(chosen):
        total = None
        for index, block in enumerate(blocks):
            copies[1 + index].wait()
            part = slice(index * block.size, (index + 1) * block.size)
            term = jnp.dot(chosen[:, part], state_ref[block, :], preferred_element_type=jnp.float32)
            total = term if total is None else total + term
        return total

    store_sums(0, sizes, live, target_ref[...], fetch, chunk_refs)


def later_sum_kernel(wave, sizes, live_ref, target_ref, state_ref, *chunk_refs):
    def fetch(chosen):
        return jnp.dot(chosen, state_ref[...], preferred_element_type=jnp.float32)

    store_sums(wave, sizes, live_ref[:, :1], target_ref[...], fetch, chunk_refs)


def chunk_shapes(wave, size, channels):
    counts = [size, size, 2 * size] if REDUCE_STEPWISE[wave] else [size] * GROUP
    return [jax.ShapeDtypeStruct((count, channels), jnp.float32) for count in counts]


def first_sums(states, targets, live, sizes):
    rows, channels = states.shape
    handed_on = [
        jax.ShapeDtypeStruct((1, LANES), jnp.int32),
        jax.ShapeDtypeStruct(targets.shape, targets.dtype),
        jax.ShapeDtypeStruct(states.shape, states.dtype),
    ]
    out = call(
        functools.partial(first_sum_kernel, sizes), chunk_shapes(0, sizes[0], channels) + handed_on, [SMEM, HBM, HBM],
        2 * sizes[0] * GROUP * rows * channels,
        [pltpu.SemaphoreType.DMA((1 + PARTS,))],
    )(live, *(pltpu.with_memory_space_constraint(value, pltpu.HBM) for value in (targets, states)))
    return out[:-3], *out[-3:]


def later_sums(states, targets, live, wave, sizes):
    rows, channels = states.shape
    return call(
        functools.partial(later_sum_kernel, wave, sizes), chunk_shapes(wave, sizes[wave], channels), [VMEM] * 3,
        2 * sizes[wave] * GROUP * rows * channels,
    )(live, targets, states)


def choose_kernel(sizes, half, live_ref, target_ref, source_ref, tie_ref, *refs):
    del tie_ref
    rows = target_ref.shape[1]
    sources = source_place(source_ref[...], half)
    pick_ref, refs = refs[0], refs[1:]
    for place, part_refs in ((target_place(target_ref[...], sizes), refs[: len(sizes)]), (sources, refs[len(sizes) :])):
        place = jnp.transpose(jnp.broadcast_to(place, (LANES, rows)))
        base = 0
        for part_ref in part_refs:
            count = part_ref.shape[1]
            for first in range(0, count, LANES):
                width = min(LANES, count - first)
                lane = lax.broadcasted_iota(jnp.int32, (rows, width), 1) + (base + first)
                part_ref[:, first : first + width] = one_hot(place[:, :width], lane)
            base += count
    sources = jnp.where(lax.broadcasted_iota(jnp.int32, (1, rows), 1) < live_ref[:, :1], sources, -1)
    pick_ref[...] = one_hot(sources, lax.broadcasted_iota(jnp.int32, pick_ref.shape, 0))


def split_sums(sum_refs, parts_ref):
    total = parts_ref.shape[0] // 3
    value = jnp.concatenate([sum_ref[...] for sum_ref in sum_refs])
    for part in range(3):
        low = value.astype(jnp.bfloat16)
        parts_ref[part * total : (part + 1) * total, :] = low
        value = value - low.astype(jnp.float32)


def gather(chosen_ref, parts_ref):
    chosen = chosen_ref[...]
    return jnp.dot(
        jnp.concatenate([chosen, chosen, chosen], axis=1), parts_ref[...], preferred_element_type=jnp.float32
    )


def gather_kernel(n_sums, *refs):
    sum_refs = refs[:n_sums]
    chosen_ref, state_ref, message_ref, parts_ref = refs[n_sums:]
    split_sums(sum_refs, parts_ref)
    message_ref[...] = gather(chosen_ref, parts_ref) - state_ref[...].astype(jnp.float32)


def gather_first(sums, chosen, states):
    rows, count = chosen.shape
    channels = sums[0].shape[1]
    return call(
        functools.partial(gather_kernel, len(sums)),
        jax.ShapeDtypeStruct((rows, channels), jnp.float32),
        [VMEM] * (len(sums) + 2), 6 * rows * count * channels,
        [pltpu.VMEM((3 * count, channels), jnp.bfloat16)],
    )(*sums, chosen, states)


def normed_activated(message_ref, chosen_ref, parts_ref, inner_ref, gain_ref):
    message = message_ref[...] + gather(chosen_ref, parts_ref)
    mean_square = jnp.mean(message * message, axis=-1, keepdims=True)
    normed = message * lax.rsqrt(mean_square + 1e-05) * gain_ref[...]
    activated = jax.nn.relu(
        jnp.dot(normed.astype(jnp.bfloat16), inner_ref[...], preferred_element_type=jnp.float32)
    ).astype(jnp.bfloat16)
    return normed, activated


def finish(normed, activated, outer_ref):
    return normed + jnp.dot(activated, outer_ref[...], preferred_element_type=jnp.float32)


def only_live(result, live_ref, first_row):
    row = lax.broadcasted_iota(jnp.int32, (result.shape[0], 1), 0) + first_row
    return jnp.where(row < live_ref[:, :1], result, jnp.float32(0.0)).astype(jnp.bfloat16)


def layer_one_kernel(n_sums, *refs):
    sum_refs = refs[:n_sums]
    message_ref, chosen_ref, pick_ref, inner_ref, outer_ref, gain_ref, reverse_ref, *piece_refs, parts_ref = refs[n_sums:]
    split_sums(sum_refs, parts_ref)
    normed, activated = normed_activated(message_ref, chosen_ref, parts_ref, inner_ref, gain_ref)
    reverse_ref[...] = finish(normed, activated, outer_ref).astype(jnp.bfloat16)
    total = jnp.dot(pick_ref[...], reverse_ref[...], preferred_element_type=jnp.float32)
    at = 0
    for piece_ref in piece_refs:
        count = piece_ref.shape[0]
        piece_ref[...] = total[at : at + count]
        at += count


def layer_two_kernel(n_sums, live_ref, *refs):
    sum_refs = refs[:n_sums]
    message_ref, chosen_ref, inner_ref, outer_ref, gain_ref, final_hbm, parts_ref, final_ref, sems = refs[n_sums:]
    split_sums(sum_refs, parts_ref)
    normed, activated = normed_activated(message_ref, chosen_ref, parts_ref, inner_ref, gain_ref)
    block = final_ref.shape[0] // 2
    copies = []
    for index in range(2):
        rows = pl.ds(index * block, block)
        part = slice(index * block, (index + 1) * block)
        final_ref[rows, :] = only_live(
            finish(normed[part], activated[part], outer_ref), live_ref, index * block
        )
        copies.append(pltpu.make_async_copy(final_ref.at[rows], final_hbm.at[rows], sems.at[index]))
        copies[-1].start()
    for copy in copies:
        copy.wait()


def swap(value, axis, mask):
    return lax.ppermute(value, axis, [(i, i ^ mask) for i in range(lax.axis_size(axis))])


def swap_group(value, kind):
    across = lax.axis_size("tgt")
    return lax.ppermute(
        value,
        ("src", "tgt"),
        [
            (i * across + j, (i ^ partner_mask(kind, j % 2)) * across + j)
            for i in range(lax.axis_size("src"))
            for j in range(across)
        ],
    )


def higher_masks(axis, low):
    masks = []
    while low < lax.axis_size(axis):
        masks.append(low)
        low *= 2
    return masks


def tie(value, other):
    return lax.optimization_barrier((value, other))[0]


def spread(total, stepwise):
    if not stepwise:
        return [total] + [swap_group(total, kind) for kind in (NEAR, FAR, BOTH)]
    near = swap_group(total, NEAR)
    return [total, near, swap_group(jnp.concatenate([total, near]), FAR)]


def reduce(chunks, stepwise, ready):
    if not stepwise:
        parts = ready([swap_group(chunks[kind], kind) for kind in (BOTH, NEAR, FAR)])
        return chunks[0] + parts[0] + parts[1] + parts[2]
    size = chunks[0].shape[0]
    part = swap_group(chunks[2], FAR)
    return chunks[0] + part[:size] + ready(swap_group(chunks[1] + part[size:], NEAR))


def target_totals(waves, between):
    first = reduce(waves[0], REDUCE_STEPWISE[0], lambda parts: parts)
    made = between(first)
    second = reduce(waves[1], REDUCE_STEPWISE[1], lambda parts: tie(parts, made))
    sums = [first, second]
    for mask in higher_masks("src", GROUP):
        parts = [swap(value, "src", mask) for value in sums]
        first = sums[0] + tie(parts[0], sums[1])
        sums = [first, sums[1] + tie(parts[1], first)]
    return [spread(value, stepwise) for value, stepwise in zip(sums, SPREAD_STEPWISE)], made


def source_totals(pieces):
    own = [mine + swap(theirs, "tgt", 1) for mine, theirs in pieces]
    for mask in higher_masks("tgt", 2):
        own = [value + swap(value, "tgt", mask) for value in own]
    return [[value, swap(value, "tgt", 1)] for value in own]


def body(
    edge_state,
    edge_source,
    edge_target,
    live_edges,
    inner_one,
    outer_one,
    inner_two,
    outer_two,
    gain_one,
    gain_two,
):
    rows, channels = edge_state.shape[2:]
    states = edge_state.reshape(rows, channels)
    sources = edge_source.reshape(1, rows)
    targets = edge_target.reshape(1, rows)
    target_atoms = ATOM_DEV * lax.axis_size("src")
    source_atoms = ATOM_DEV * lax.axis_size("tgt")
    sizes = wave_sizes(target_atoms)
    half = source_atoms // 2
    first, live, targets, states = first_sums(states, targets, live_edges, sizes)
    waves = [first] + [later_sums(states, targets, live, wave, sizes) for wave in range(1, len(sizes))]

    pieces = piece_sizes(half)
    n_waves = len(sizes)

    def choose(first):
        return call(
            functools.partial(choose_kernel, sizes, half),
            [jax.ShapeDtypeStruct((source_atoms, rows), jnp.bfloat16)]
            + [jax.ShapeDtypeStruct((rows, GROUP * size), jnp.bfloat16) for size in sizes]
            + [jax.ShapeDtypeStruct((rows, 2 * size), jnp.bfloat16) for size in pieces],
            [VMEM] * 4, HIDE_FLOPS,
        )(live, targets, sources, first)

    totals, (source_pick, *chosen) = target_totals(waves, choose)
    target_chosen, source_chosen = chosen[:n_waves], chosen[n_waves:]
    message = gather_first(totals[0], target_chosen[0], states)
    reverse_state, *sums = call(
        functools.partial(layer_one_kernel, len(totals[1])),
        [jax.ShapeDtypeStruct((rows, channels), jnp.bfloat16)]
        + [jax.ShapeDtypeStruct((size, channels), jnp.float32) for size in pieces for _ in range(2)],
        [VMEM] * (len(totals[1]) + 6),
        2 * rows * channels * (3 * GROUP * sizes[1] + 2 * channels + source_atoms),
        [pltpu.VMEM((3 * GROUP * sizes[1], channels), jnp.bfloat16)],
    )(*totals[1], message, target_chosen[1], source_pick, inner_one, outer_one, gain_one.reshape(1, channels))
    totals = source_totals(list(zip(sums[::2], sums[1::2])))
    message = gather_first(totals[0], source_chosen[0], reverse_state)
    final_state = call(
        functools.partial(layer_two_kernel, len(totals[1])),
        jax.ShapeDtypeStruct((rows, channels), jnp.bfloat16),
        [VMEM] * (len(totals[1]) + 6),
        2 * rows * channels * (6 * pieces[1] + 2 * channels),
        [
            pltpu.VMEM((6 * pieces[1], channels), jnp.bfloat16),
            pltpu.VMEM((rows, channels), jnp.bfloat16),
            pltpu.SemaphoreType.DMA((2,)),
        ],
        HBM,
    )(live, *totals[1], message, source_chosen[1], inner_two, outer_two, gain_two.reshape(1, channels))
    return final_state.reshape(1, 1, rows, channels)


def solution(mesh):
    placed = (
        P("src", "tgt", None, None),
        P("src", "tgt", None),
        P("src", "tgt", None),
        P("src", "tgt"),
        P(),
        P(),
        P(),
        P(),
        P(),
        P(),
    )
    return jax.shard_map(
        body, mesh=mesh, in_specs=placed, out_specs=P("src", "tgt", None, None), check_vma=False
    )
```

```python
import functools

import jax
import jax.numpy as jnp
from jax import lax
from jax.experimental import pallas as pl
from jax.experimental.pallas import tpu as pltpu
from jax.sharding import PartitionSpec as P

ATOM_DEV = 64
GROUP = 4
NEAR, FAR, BOTH = 1, 2, 3
SHARES = (4, 4)
REDUCE_STEPWISE = (False, True)
SPREAD_STEPWISE = (False, False)
PIECES = (1, 1)
PARTS = 2
LANES = 128
HIDE_FLOPS = 8 * 10**9
VMEM_LIMIT = 40 * 1024 * 1024

VMEM = pl.BlockSpec(memory_space=pltpu.VMEM)
HBM = pl.BlockSpec(memory_space=pltpu.HBM)
SMEM = pl.BlockSpec(memory_space=pltpu.SMEM)


def call(kernel, out_shape, in_specs, flops, scratch=(), out_specs=None):
    return pl.pallas_call(
        kernel,
        out_shape=out_shape,
        in_specs=in_specs,
        out_specs=jax.tree.map(lambda _: VMEM, out_shape) if out_specs is None else out_specs,
        scratch_shapes=list(scratch),
        compiler_params=pltpu.CompilerParams(vmem_limit_bytes=VMEM_LIMIT),
        cost_estimate=pl.CostEstimate(flops=flops, bytes_accessed=0, transcendentals=0),
    )


def wave_sizes(atoms):
    return [atoms // (GROUP * sum(SHARES)) * share for share in SHARES]


def partner_mask(kind, core):
    if kind in (NEAR, FAR) and core == 0:
        return NEAR + FAR - kind
    return kind


def target_place(atoms, sizes):
    device = lax.axis_index("src")
    low, high = device % 2, (device // 2) % 2
    own = jnp.where(lax.axis_index("tgt") % 2 == 0, high + 2 * low, low + 2 * high)
    place = atoms
    base = 0
    for size in sizes:
        inside = atoms - base
        chunk = sum((inside >= k * size).astype(jnp.int32) for k in range(1, GROUP))
        spot = base + jnp.bitwise_xor(chunk, own) * size + inside - chunk * size
        place = jnp.where(inside >= 0, spot, place)
        base += GROUP * size
    return place


def piece_sizes(half):
    return [half // sum(PIECES) * piece for piece in PIECES]


def source_place(atoms, half):
    own = (lax.axis_index("tgt") % 2) * half
    ours = jnp.bitwise_xor(atoms, own)
    other = (ours >= half).astype(jnp.int32)
    inside = ours - other * half
    place = atoms
    base = 0
    for size in piece_sizes(half):
        place = jnp.where(inside >= base, 2 * base + other * size + inside - base, place)
        base += size
    return place


def one_hot(place, slot):
    return jnp.where(place == slot, jnp.float32(1.0), jnp.float32(0.0)).astype(jnp.bfloat16)


def store_sums(wave, sizes, live, targets, fetch, chunk_refs):
    rows = targets.shape[1]
    size = sizes[wave]
    place = target_place(targets, sizes)
    place = jnp.where(lax.broadcasted_iota(jnp.int32, (1, rows), 1) < live, place, -1)
    slot = lax.broadcasted_iota(jnp.int32, (size * GROUP, rows), 0) + sum(sizes[:wave]) * GROUP
    chosen = one_hot(place, slot)
    total = fetch(chosen)
    at = 0
    for chunk_ref in chunk_refs:
        count = chunk_ref.shape[0]
        chunk_ref[...] = total[at : at + count]
        at += count


def first_sum_kernel(sizes, live_ref, target_hbm, state_hbm, *refs):
    *chunk_refs, live_out, target_ref, state_ref, sems = refs
    rows = state_ref.shape[0]
    blocks = [pl.ds(first, rows // PARTS) for first in range(0, rows, rows // PARTS)]
    copies = [
        pltpu.make_async_copy(source, place, sems.at[index])
        for index, (source, place) in enumerate(
            [(target_hbm, target_ref)] + [(state_hbm.at[block], state_ref.at[block]) for block in blocks]
        )
    ]
    for copy in copies:
        copy.start()
    live = live_ref[0, 0]
    live_out[...] = jnp.full(live_out.shape, live, jnp.int32)
    copies[0].wait()

    def fetch(chosen):
        total = None
        for index, block in enumerate(blocks):
            copies[1 + index].wait()
            part = slice(index * block.size, (index + 1) * block.size)
            term = jnp.dot(chosen[:, part], state_ref[block, :], preferred_element_type=jnp.float32)
            total = term if total is None else total + term
        return total

    store_sums(0, sizes, live, target_ref[...], fetch, chunk_refs)


def later_sum_kernel(wave, sizes, live_ref, target_ref, state_ref, *chunk_refs):
    def fetch(chosen):
        return jnp.dot(chosen, state_ref[...], preferred_element_type=jnp.float32)

    store_sums(wave, sizes, live_ref[:, :1], target_ref[...], fetch, chunk_refs)


def chunk_shapes(wave, size, channels):
    counts = [size, size, 2 * size] if REDUCE_STEPWISE[wave] else [size] * GROUP
    return [jax.ShapeDtypeStruct((count, channels), jnp.float32) for count in counts]


def first_sums(states, targets, live, sizes):
    rows, channels = states.shape
    handed_on = [
        jax.ShapeDtypeStruct((1, LANES), jnp.int32),
        jax.ShapeDtypeStruct(targets.shape, targets.dtype),
        jax.ShapeDtypeStruct(states.shape, states.dtype),
    ]
    out = call(
        functools.partial(first_sum_kernel, sizes), chunk_shapes(0, sizes[0], channels) + handed_on, [SMEM, HBM, HBM],
        2 * sizes[0] * GROUP * rows * channels,
        [pltpu.SemaphoreType.DMA((1 + PARTS,))],
    )(live, *(pltpu.with_memory_space_constraint(value, pltpu.HBM) for value in (targets, states)))
    return out[:-3], *out[-3:]


def later_sums(states, targets, live, wave, sizes):
    rows, channels = states.shape
    return call(
        functools.partial(later_sum_kernel, wave, sizes), chunk_shapes(wave, sizes[wave], channels), [VMEM] * 3,
        2 * sizes[wave] * GROUP * rows * channels,
    )(live, targets, states)


def choose_kernel(sizes, half, live_ref, target_ref, source_ref, tie_ref, pick_ref, *refs):
    del tie_ref
    rows = target_ref.shape[1]
    sources = source_place(source_ref[...], half)
    for place, part_refs in ((target_place(target_ref[...], sizes), refs[:2]), (sources, refs[2:])):
        place = jnp.transpose(jnp.broadcast_to(place, (LANES, rows)))
        base = 0
        for part_ref in part_refs:
            columns = part_ref.shape[1]
            count = columns // 3
            for first in range(0, columns, LANES):
                width = min(LANES, columns - first)
                slot = (lax.broadcasted_iota(jnp.int32, (1, width), 1) + first) % count + base
                part_ref[:, first : first + width] = one_hot(place[:, :width], slot)
            base += count
    sources = jnp.where(lax.broadcasted_iota(jnp.int32, (1, rows), 1) < live_ref[:, :1], sources, -1)
    pick_ref[...] = one_hot(sources, lax.broadcasted_iota(jnp.int32, pick_ref.shape, 0))


def split_sums(sum_refs, parts_ref):
    total = parts_ref.shape[0] // 3
    value = jnp.concatenate([sum_ref[...] for sum_ref in sum_refs])
    for part in range(3):
        low = value.astype(jnp.bfloat16)
        parts_ref[part * total : (part + 1) * total, :] = low
        value = value - low.astype(jnp.float32)


def gather(chosen_ref, parts_ref):
    return jnp.dot(chosen_ref[...], parts_ref[...], preferred_element_type=jnp.float32)


def gather_kernel(n_sums, *refs):
    sum_refs = refs[:n_sums]
    chosen_ref, state_ref, message_ref, parts_ref = refs[n_sums:]
    split_sums(sum_refs, parts_ref)
    message_ref[...] = gather(chosen_ref, parts_ref) - state_ref[...].astype(jnp.float32)


def gather_first(sums, chosen, states):
    rows, columns = chosen.shape
    channels = sums[0].shape[1]
    return call(
        functools.partial(gather_kernel, len(sums)),
        jax.ShapeDtypeStruct((rows, channels), jnp.float32),
        [VMEM] * (len(sums) + 2), 2 * rows * columns * channels,
        [pltpu.VMEM((columns, channels), jnp.bfloat16)],
    )(*sums, chosen, states)


def normed_activated(message_ref, chosen_ref, parts_ref, inner_ref, gain_ref):
    message = message_ref[...] + gather(chosen_ref, parts_ref)
    mean_square = jnp.mean(message * message, axis=-1, keepdims=True)
    normed = message * lax.rsqrt(mean_square + 1e-05) * gain_ref[...]
    activated = jax.nn.relu(
        jnp.dot(normed.astype(jnp.bfloat16), inner_ref[...], preferred_element_type=jnp.float32)
    ).astype(jnp.bfloat16)
    return normed, activated


def finish(normed, activated, outer_ref):
    return normed + jnp.dot(activated, outer_ref[...], preferred_element_type=jnp.float32)


def only_live(result, live_ref, first_row):
    row = lax.broadcasted_iota(jnp.int32, (result.shape[0], 1), 0) + first_row
    return jnp.where(row < live_ref[:, :1], result, jnp.float32(0.0)).astype(jnp.bfloat16)


def layer_one_kernel(n_sums, *refs):
    sum_refs = refs[:n_sums]
    message_ref, chosen_ref, pick_ref, inner_ref, outer_ref, gain_ref, reverse_ref, *piece_refs, parts_ref = refs[n_sums:]
    split_sums(sum_refs, parts_ref)
    normed, activated = normed_activated(message_ref, chosen_ref, parts_ref, inner_ref, gain_ref)
    reverse_ref[...] = finish(normed, activated, outer_ref).astype(jnp.bfloat16)
    total = jnp.dot(pick_ref[...], reverse_ref[...], preferred_element_type=jnp.float32)
    at = 0
    for piece_ref in piece_refs:
        count = piece_ref.shape[0]
        piece_ref[...] = total[at : at + count]
        at += count


def layer_two_kernel(n_sums, live_ref, *refs):
    sum_refs = refs[:n_sums]
    message_ref, chosen_ref, inner_ref, outer_ref, gain_ref, final_hbm, parts_ref, final_ref, sems = refs[n_sums:]
    split_sums(sum_refs, parts_ref)
    normed, activated = normed_activated(message_ref, chosen_ref, parts_ref, inner_ref, gain_ref)
    block = final_ref.shape[0] // 4
    copies = []
    for index in range(4):
        rows = pl.ds(index * block, block)
        part = slice(index * block, (index + 1) * block)
        final_ref[rows, :] = only_live(
            finish(normed[part], activated[part], outer_ref), live_ref, index * block
        )
        copies.append(pltpu.make_async_copy(final_ref.at[rows], final_hbm.at[rows], sems.at[index]))
        copies[-1].start()
    for copy in copies:
        copy.wait()


def swap(value, axis, mask):
    return lax.ppermute(value, axis, [(i, i ^ mask) for i in range(lax.axis_size(axis))])


def swap_group(value, kind):
    across = lax.axis_size("tgt")
    return lax.ppermute(
        value,
        ("src", "tgt"),
        [
            (i * across + j, (i ^ partner_mask(kind, j % 2)) * across + j)
            for i in range(lax.axis_size("src"))
            for j in range(across)
        ],
    )


def higher_masks(axis, low):
    masks = []
    while low < lax.axis_size(axis):
        masks.append(low)
        low *= 2
    return masks


def tie(value, other):
    return lax.optimization_barrier((value, other))[0]


def spread(total, stepwise):
    if not stepwise:
        return [total] + [swap_group(total, kind) for kind in (NEAR, FAR, BOTH)]
    near = swap_group(total, NEAR)
    return [total, near, swap_group(jnp.concatenate([total, near]), FAR)]


def reduce(chunks, stepwise, ready):
    if not stepwise:
        parts = ready([swap_group(chunks[kind], kind) for kind in (BOTH, NEAR, FAR)])
        return chunks[0] + parts[0] + parts[1] + parts[2]
    size = chunks[0].shape[0]
    part = swap_group(chunks[2], FAR)
    return chunks[0] + part[:size] + ready(swap_group(chunks[1] + part[size:], NEAR))


def target_totals(waves, between):
    first = reduce(waves[0], REDUCE_STEPWISE[0], lambda parts: parts)
    made = between(first)
    second = reduce(waves[1], REDUCE_STEPWISE[1], lambda parts: tie(parts, made))
    sums = [first, second]
    for mask in higher_masks("src", GROUP):
        parts = [swap(value, "src", mask) for value in sums]
        first = sums[0] + tie(parts[0], sums[1])
        sums = [first, sums[1] + tie(parts[1], first)]
    return [spread(value, stepwise) for value, stepwise in zip(sums, SPREAD_STEPWISE)], made


def source_totals(pieces):
    own = [mine + swap(theirs, "tgt", 1) for mine, theirs in pieces]
    for mask in higher_masks("tgt", 2):
        own = [value + swap(value, "tgt", mask) for value in own]
    return [[value, swap(value, "tgt", 1)] for value in own]


def body(
    edge_state,
    edge_source,
    edge_target,
    live_edges,
    inner_one,
    outer_one,
    inner_two,
    outer_two,
    gain_one,
    gain_two,
):
    rows, channels = edge_state.shape[2:]
    states = edge_state.reshape(rows, channels)
    sources = edge_source.reshape(1, rows)
    targets = edge_target.reshape(1, rows)
    target_atoms = ATOM_DEV * lax.axis_size("src")
    source_atoms = ATOM_DEV * lax.axis_size("tgt")
    sizes = wave_sizes(target_atoms)
    half = source_atoms // 2
    first, live, targets, states = first_sums(states, targets, live_edges, sizes)
    waves = [first] + [later_sums(states, targets, live, wave, sizes) for wave in range(1, len(sizes))]

    pieces = piece_sizes(half)
    parts = (
        GROUP * sizes[0] + sizes[1], (GROUP - 1) * sizes[1], 2 * pieces[0] + pieces[1], pieces[1]
    )

    def choose(first):
        return call(
            functools.partial(choose_kernel, sizes, half),
            [jax.ShapeDtypeStruct((source_atoms, rows), jnp.bfloat16)]
            + [jax.ShapeDtypeStruct((rows, 3 * count), jnp.bfloat16) for count in parts],
            [VMEM] * 4, HIDE_FLOPS,
        )(live, targets, sources, first)

    totals, (source_pick, *chosen) = target_totals(waves, choose)
    early, late = totals[0] + totals[1][:1], totals[1][1:]
    message = gather_first(early, chosen[0], states)
    reverse_state, *sums = call(
        functools.partial(layer_one_kernel, len(late)),
        [jax.ShapeDtypeStruct((rows, channels), jnp.bfloat16)]
        + [jax.ShapeDtypeStruct((size, channels), jnp.float32) for size in pieces for _ in range(2)],
        [VMEM] * (len(late) + 6),
        2 * rows * channels * (3 * parts[1] + 2 * channels + source_atoms),
        [pltpu.VMEM((3 * parts[1], channels), jnp.bfloat16)],
    )(*late, message, chosen[1], source_pick, inner_one, outer_one, gain_one.reshape(1, channels))
    totals = source_totals(list(zip(sums[::2], sums[1::2])))
    early, late = totals[0] + totals[1][:1], totals[1][1:]
    message = gather_first(early, chosen[2], reverse_state)
    final_state = call(
        functools.partial(layer_two_kernel, len(late)),
        jax.ShapeDtypeStruct((rows, channels), jnp.bfloat16),
        [VMEM] * (len(late) + 6),
        2 * rows * channels * (3 * parts[3] + 2 * channels),
        [
            pltpu.VMEM((3 * parts[3], channels), jnp.bfloat16),
            pltpu.VMEM((rows, channels), jnp.bfloat16),
            pltpu.SemaphoreType.DMA((4,)),
        ],
        HBM,
    )(live, *late, message, chosen[3], inner_two, outer_two, gain_two.reshape(1, channels))
    return final_state.reshape(1, 1, rows, channels)


def solution(mesh):
    placed = (
        P("src", "tgt", None, None),
        P("src", "tgt", None),
        P("src", "tgt", None),
        P("src", "tgt"),
        P(),
        P(),
        P(),
        P(),
        P(),
        P(),
    )
    return jax.shard_map(
        body, mesh=mesh, in_specs=placed, out_specs=P("src", "tgt", None, None), check_vma=False
    )
```

```python
import functools

import jax
import jax.numpy as jnp
from jax import lax
from jax.experimental import pallas as pl
from jax.experimental.pallas import tpu as pltpu
from jax.sharding import PartitionSpec as P

ATOM_DEV = 64
GROUP = 4
NEAR, FAR, BOTH = 1, 2, 3
SHARES = (4, 4)
REDUCE_STEPWISE = (False, True)
SPREAD_STEPWISE = (False, False)
PIECES = (1, 1)
PARTS = 4
LANES = 128
HIDE_FLOPS = 8 * 10**9
VMEM_LIMIT = 40 * 1024 * 1024

VMEM = pl.BlockSpec(memory_space=pltpu.VMEM)
HBM = pl.BlockSpec(memory_space=pltpu.HBM)
SMEM = pl.BlockSpec(memory_space=pltpu.SMEM)


def call(kernel, out_shape, in_specs, flops, scratch=(), out_specs=None):
    return pl.pallas_call(
        kernel,
        out_shape=out_shape,
        in_specs=in_specs,
        out_specs=jax.tree.map(lambda _: VMEM, out_shape) if out_specs is None else out_specs,
        scratch_shapes=list(scratch),
        compiler_params=pltpu.CompilerParams(vmem_limit_bytes=VMEM_LIMIT),
        cost_estimate=pl.CostEstimate(flops=flops, bytes_accessed=0, transcendentals=0),
    )


def wave_sizes(atoms):
    return [atoms // (GROUP * sum(SHARES)) * share for share in SHARES]


def partner_mask(kind, core):
    if kind in (NEAR, FAR) and core == 0:
        return NEAR + FAR - kind
    return kind


def target_place(atoms, sizes):
    device = lax.axis_index("src")
    low, high = device % 2, (device // 2) % 2
    own = jnp.where(lax.axis_index("tgt") % 2 == 0, high + 2 * low, low + 2 * high)
    place = atoms
    base = 0
    for size in sizes:
        inside = atoms - base
        chunk = sum((inside >= k * size).astype(jnp.int32) for k in range(1, GROUP))
        spot = base + jnp.bitwise_xor(chunk, own) * size + inside - chunk * size
        place = jnp.where(inside >= 0, spot, place)
        base += GROUP * size
    return place


def piece_sizes(half):
    return [half // sum(PIECES) * piece for piece in PIECES]


def source_place(atoms, half):
    own = (lax.axis_index("tgt") % 2) * half
    ours = jnp.bitwise_xor(atoms, own)
    other = (ours >= half).astype(jnp.int32)
    inside = ours - other * half
    place = atoms
    base = 0
    for size in piece_sizes(half):
        place = jnp.where(inside >= base, 2 * base + other * size + inside - base, place)
        base += size
    return place


def one_hot(place, slot):
    return jnp.where(place == slot, jnp.float32(1.0), jnp.float32(0.0)).astype(jnp.bfloat16)


def store_sums(wave, sizes, live, targets, fetch, chunk_refs):
    rows = targets.shape[1]
    size = sizes[wave]
    place = target_place(targets, sizes)
    place = jnp.where(lax.broadcasted_iota(jnp.int32, (1, rows), 1) < live, place, -1)
    slot = lax.broadcasted_iota(jnp.int32, (size * GROUP, rows), 0) + sum(sizes[:wave]) * GROUP
    chosen = one_hot(place, slot)
    total = fetch(chosen)
    at = 0
    for chunk_ref in chunk_refs:
        count = chunk_ref.shape[0]
        chunk_ref[...] = total[at : at + count]
        at += count


def first_sum_kernel(sizes, live_ref, target_hbm, state_hbm, *refs):
    *chunk_refs, live_out, target_ref, state_ref, sems = refs
    rows = state_ref.shape[0]
    blocks = [pl.ds(first, rows // PARTS) for first in range(0, rows, rows // PARTS)]
    copies = [
        pltpu.make_async_copy(source, place, sems.at[index])
        for index, (source, place) in enumerate(
            [(target_hbm, target_ref)] + [(state_hbm.at[block], state_ref.at[block]) for block in blocks]
        )
    ]
    for copy in copies:
        copy.start()
    live = live_ref[0, 0]
    live_out[...] = jnp.full(live_out.shape, live, jnp.int32)
    copies[0].wait()

    def fetch(chosen):
        total = None
        for index, block in enumerate(blocks):
            copies[1 + index].wait()
            part = slice(index * block.size, (index + 1) * block.size)
            term = jnp.dot(chosen[:, part], state_ref[block, :], preferred_element_type=jnp.float32)
            total = term if total is None else total + term
        return total

    store_sums(0, sizes, live, target_ref[...], fetch, chunk_refs)


def later_sum_kernel(wave, sizes, live_ref, target_ref, state_ref, *chunk_refs):
    def fetch(chosen):
        return jnp.dot(chosen, state_ref[...], preferred_element_type=jnp.float32)

    store_sums(wave, sizes, live_ref[:, :1], target_ref[...], fetch, chunk_refs)


def chunk_shapes(wave, size, channels):
    counts = [size, size, 2 * size] if REDUCE_STEPWISE[wave] else [size] * GROUP
    return [jax.ShapeDtypeStruct((count, channels), jnp.float32) for count in counts]


def first_sums(states, targets, live, sizes):
    rows, channels = states.shape
    handed_on = [
        jax.ShapeDtypeStruct((1, LANES), jnp.int32),
        jax.ShapeDtypeStruct(targets.shape, targets.dtype),
        jax.ShapeDtypeStruct(states.shape, states.dtype),
    ]
    out = call(
        functools.partial(first_sum_kernel, sizes), chunk_shapes(0, sizes[0], channels) + handed_on, [SMEM, HBM, HBM],
        2 * sizes[0] * GROUP * rows * channels,
        [pltpu.SemaphoreType.DMA((1 + PARTS,))],
    )(live, *(pltpu.with_memory_space_constraint(value, pltpu.HBM) for value in (targets, states)))
    return out[:-3], *out[-3:]


def later_sums(states, targets, live, wave, sizes):
    rows, channels = states.shape
    return call(
        functools.partial(later_sum_kernel, wave, sizes), chunk_shapes(wave, sizes[wave], channels), [VMEM] * 3,
        2 * sizes[wave] * GROUP * rows * channels,
    )(live, targets, states)


def choose_kernel(sizes, half, live_ref, target_ref, source_ref, tie_ref, pick_ref, *refs):
    del tie_ref
    rows = target_ref.shape[1]
    sources = source_place(source_ref[...], half)
    for place, part_refs in ((target_place(target_ref[...], sizes), refs[:2]), (sources, refs[2:])):
        place = jnp.transpose(jnp.broadcast_to(place, (LANES, rows)))
        base = 0
        for part_ref in part_refs:
            columns = part_ref.shape[1]
            count = columns // 3
            for first in range(0, columns, LANES):
                width = min(LANES, columns - first)
                slot = (lax.broadcasted_iota(jnp.int32, (1, width), 1) + first) % count + base
                part_ref[:, first : first + width] = one_hot(place[:, :width], slot)
            base += count
    sources = jnp.where(lax.broadcasted_iota(jnp.int32, (1, rows), 1) < live_ref[:, :1], sources, -1)
    pick_ref[...] = one_hot(sources, lax.broadcasted_iota(jnp.int32, pick_ref.shape, 0))


def split_sums(sum_refs, parts_ref):
    total = parts_ref.shape[0] // 3
    value = jnp.concatenate([sum_ref[...] for sum_ref in sum_refs])
    for part in range(3):
        low = value.astype(jnp.bfloat16)
        parts_ref[part * total : (part + 1) * total, :] = low
        value = value - low.astype(jnp.float32)


def gather(chosen_ref, parts_ref):
    return jnp.dot(chosen_ref[...], parts_ref[...], preferred_element_type=jnp.float32)


def gather_kernel(n_sums, *refs):
    sum_refs = refs[:n_sums]
    chosen_ref, state_ref, message_ref, parts_ref = refs[n_sums:]
    split_sums(sum_refs, parts_ref)
    message_ref[...] = gather(chosen_ref, parts_ref) - state_ref[...].astype(jnp.float32)


def gather_first(sums, chosen, states):
    rows, columns = chosen.shape
    channels = sums[0].shape[1]
    return call(
        functools.partial(gather_kernel, len(sums)),
        jax.ShapeDtypeStruct((rows, channels), jnp.float32),
        [VMEM] * (len(sums) + 2), 2 * rows * columns * channels,
        [pltpu.VMEM((columns, channels), jnp.bfloat16)],
    )(*sums, chosen, states)


def normed_activated(message_ref, chosen_ref, parts_ref, inner_ref, gain_ref):
    message = message_ref[...] + gather(chosen_ref, parts_ref)
    mean_square = jnp.mean(message * message, axis=-1, keepdims=True)
    normed = message * lax.rsqrt(mean_square + 1e-05) * gain_ref[...]
    activated = jax.nn.relu(
        jnp.dot(normed.astype(jnp.bfloat16), inner_ref[...], preferred_element_type=jnp.float32)
    ).astype(jnp.bfloat16)
    return normed, activated


def finish(normed, activated, outer_ref):
    return normed + jnp.dot(activated, outer_ref[...], preferred_element_type=jnp.float32)


def only_live(result, live_ref, first_row):
    row = lax.broadcasted_iota(jnp.int32, (result.shape[0], 1), 0) + first_row
    return jnp.where(row < live_ref[:, :1], result, jnp.float32(0.0)).astype(jnp.bfloat16)


def layer_one_kernel(n_sums, *refs):
    sum_refs = refs[:n_sums]
    message_ref, chosen_ref, pick_ref, inner_ref, outer_ref, gain_ref, reverse_ref, *piece_refs, parts_ref = refs[n_sums:]
    split_sums(sum_refs, parts_ref)
    normed, activated = normed_activated(message_ref, chosen_ref, parts_ref, inner_ref, gain_ref)
    reverse_ref[...] = finish(normed, activated, outer_ref).astype(jnp.bfloat16)
    total = jnp.dot(pick_ref[...], reverse_ref[...], preferred_element_type=jnp.float32)
    at = 0
    for piece_ref in piece_refs:
        count = piece_ref.shape[0]
        piece_ref[...] = total[at : at + count]
        at += count


def layer_two_kernel(n_sums, live_ref, *refs):
    sum_refs = refs[:n_sums]
    message_ref, chosen_ref, inner_ref, outer_ref, gain_ref, final_hbm, parts_ref, final_ref, sems = refs[n_sums:]
    split_sums(sum_refs, parts_ref)
    normed, activated = normed_activated(message_ref, chosen_ref, parts_ref, inner_ref, gain_ref)
    block = final_ref.shape[0] // 4
    copies = []
    for index in range(4):
        rows = pl.ds(index * block, block)
        part = slice(index * block, (index + 1) * block)
        final_ref[rows, :] = only_live(
            finish(normed[part], activated[part], outer_ref), live_ref, index * block
        )
        copies.append(pltpu.make_async_copy(final_ref.at[rows], final_hbm.at[rows], sems.at[index]))
        copies[-1].start()
    for copy in copies:
        copy.wait()


def swap(value, axis, mask):
    return lax.ppermute(value, axis, [(i, i ^ mask) for i in range(lax.axis_size(axis))])


def swap_group(value, kind):
    across = lax.axis_size("tgt")
    return lax.ppermute(
        value,
        ("src", "tgt"),
        [
            (i * across + j, (i ^ partner_mask(kind, j % 2)) * across + j)
            for i in range(lax.axis_size("src"))
            for j in range(across)
        ],
    )


def higher_masks(axis, low):
    masks = []
    while low < lax.axis_size(axis):
        masks.append(low)
        low *= 2
    return masks


def tie(value, other):
    return lax.optimization_barrier((value, other))[0]


def spread(total, stepwise):
    if not stepwise:
        return [total] + [swap_group(total, kind) for kind in (NEAR, FAR, BOTH)]
    near = swap_group(total, NEAR)
    return [total, near, swap_group(jnp.concatenate([total, near]), FAR)]


def reduce(chunks, stepwise, ready):
    if not stepwise:
        parts = ready([swap_group(chunks[kind], kind) for kind in (BOTH, NEAR, FAR)])
        return chunks[0] + parts[0] + parts[1] + parts[2]
    size = chunks[0].shape[0]
    part = swap_group(chunks[2], FAR)
    return chunks[0] + part[:size] + ready(swap_group(chunks[1] + part[size:], NEAR))


def target_totals(waves, between):
    first = reduce(waves[0], REDUCE_STEPWISE[0], lambda parts: parts)
    made = between(first)
    second = reduce(waves[1], REDUCE_STEPWISE[1], lambda parts: tie(parts, made))
    sums = [first, second]
    for mask in higher_masks("src", GROUP):
        parts = [swap(value, "src", mask) for value in sums]
        first = sums[0] + tie(parts[0], sums[1])
        sums = [first, sums[1] + tie(parts[1], first)]
    return [spread(value, stepwise) for value, stepwise in zip(sums, SPREAD_STEPWISE)], made


def source_totals(pieces):
    own = [mine + swap(theirs, "tgt", 1) for mine, theirs in pieces]
    for mask in higher_masks("tgt", 2):
        own = [value + swap(value, "tgt", mask) for value in own]
    return [[value, swap(value, "tgt", 1)] for value in own]


def body(
    edge_state,
    edge_source,
    edge_target,
    live_edges,
    inner_one,
    outer_one,
    inner_two,
    outer_two,
    gain_one,
    gain_two,
):
    rows, channels = edge_state.shape[2:]
    states = edge_state.reshape(rows, channels)
    sources = edge_source.reshape(1, rows)
    targets = edge_target.reshape(1, rows)
    target_atoms = ATOM_DEV * lax.axis_size("src")
    source_atoms = ATOM_DEV * lax.axis_size("tgt")
    sizes = wave_sizes(target_atoms)
    half = source_atoms // 2
    first, live, targets, states = first_sums(states, targets, live_edges, sizes)
    waves = [first] + [later_sums(states, targets, live, wave, sizes) for wave in range(1, len(sizes))]

    pieces = piece_sizes(half)
    parts = (
        GROUP * sizes[0] + sizes[1], (GROUP - 1) * sizes[1], 2 * pieces[0] + pieces[1], pieces[1]
    )

    def choose(first):
        return call(
            functools.partial(choose_kernel, sizes, half),
            [jax.ShapeDtypeStruct((source_atoms, rows), jnp.bfloat16)]
            + [jax.ShapeDtypeStruct((rows, 3 * count), jnp.bfloat16) for count in parts],
            [VMEM] * 4, HIDE_FLOPS,
        )(live, targets, sources, first)

    totals, (source_pick, *chosen) = target_totals(waves, choose)
    early, late = totals[0] + totals[1][:1], totals[1][1:]
    message = gather_first(early, chosen[0], states)
    reverse_state, *sums = call(
        functools.partial(layer_one_kernel, len(late)),
        [jax.ShapeDtypeStruct((rows, channels), jnp.bfloat16)]
        + [jax.ShapeDtypeStruct((size, channels), jnp.float32) for size in pieces for _ in range(2)],
        [VMEM] * (len(late) + 6),
        2 * rows * channels * (3 * parts[1] + 2 * channels + source_atoms),
        [pltpu.VMEM((3 * parts[1], channels), jnp.bfloat16)],
    )(*late, message, chosen[1], source_pick, inner_one, outer_one, gain_one.reshape(1, channels))
    totals = source_totals(list(zip(sums[::2], sums[1::2])))
    early, late = totals[0] + totals[1][:1], totals[1][1:]
    message = gather_first(early, chosen[2], reverse_state)
    final_state = call(
        functools.partial(layer_two_kernel, len(late)),
        jax.ShapeDtypeStruct((rows, channels), jnp.bfloat16),
        [VMEM] * (len(late) + 6),
        2 * rows * channels * (3 * parts[3] + 2 * channels),
        [
            pltpu.VMEM((3 * parts[3], channels), jnp.bfloat16),
            pltpu.VMEM((rows, channels), jnp.bfloat16),
            pltpu.SemaphoreType.DMA((4,)),
        ],
        HBM,
    )(live, *late, message, chosen[3], inner_two, outer_two, gain_two.reshape(1, channels))
    return final_state.reshape(1, 1, rows, channels)


def solution(mesh):
    placed = (
        P("src", "tgt", None, None),
        P("src", "tgt", None),
        P("src", "tgt", None),
        P("src", "tgt"),
        P(),
        P(),
        P(),
        P(),
        P(),
        P(),
    )
    return jax.shard_map(
        body, mesh=mesh, in_specs=placed, out_specs=P("src", "tgt", None, None), check_vma=False
    )
```

```python
import functools

import jax
import jax.numpy as jnp
from jax import lax
from jax.experimental import pallas as pl
from jax.experimental.pallas import tpu as pltpu
from jax.sharding import PartitionSpec as P

ATOM_DEV = 64
GROUP = 4
NEAR, FAR, BOTH = 1, 2, 3
SHARES = (4, 4)
REDUCE_STEPWISE = (False, True)
SPREAD_STEPWISE = (False, False)
PIECES = (1, 1)
PARTS = 4
LANES = 128
HIDE_FLOPS = 8 * 10**9
VMEM_LIMIT = 40 * 1024 * 1024

VMEM = pl.BlockSpec(memory_space=pltpu.VMEM)
HBM = pl.BlockSpec(memory_space=pltpu.HBM)
SMEM = pl.BlockSpec(memory_space=pltpu.SMEM)


def call(kernel, out_shape, in_specs, flops, scratch=(), out_specs=None):
    return pl.pallas_call(
        kernel,
        out_shape=out_shape,
        in_specs=in_specs,
        out_specs=jax.tree.map(lambda _: VMEM, out_shape) if out_specs is None else out_specs,
        scratch_shapes=list(scratch),
        compiler_params=pltpu.CompilerParams(vmem_limit_bytes=VMEM_LIMIT),
        cost_estimate=pl.CostEstimate(flops=flops, bytes_accessed=0, transcendentals=0),
    )


def wave_sizes(atoms):
    return [atoms // (GROUP * sum(SHARES)) * share for share in SHARES]


def partner_mask(kind, core):
    if kind in (NEAR, FAR) and core == 0:
        return NEAR + FAR - kind
    return kind


def target_place(atoms, sizes):
    device = lax.axis_index("src")
    low, high = device % 2, (device // 2) % 2
    own = jnp.where(lax.axis_index("tgt") % 2 == 0, high + 2 * low, low + 2 * high)
    place = atoms
    base = 0
    for size in sizes:
        inside = atoms - base
        chunk = sum((inside >= k * size).astype(jnp.int32) for k in range(1, GROUP))
        spot = base + jnp.bitwise_xor(chunk, own) * size + inside - chunk * size
        place = jnp.where(inside >= 0, spot, place)
        base += GROUP * size
    return place


def piece_sizes(half):
    return [half // sum(PIECES) * piece for piece in PIECES]


def source_place(atoms, half):
    own = (lax.axis_index("tgt") % 2) * half
    ours = jnp.bitwise_xor(atoms, own)
    other = (ours >= half).astype(jnp.int32)
    inside = ours - other * half
    place = atoms
    base = 0
    for size in piece_sizes(half):
        place = jnp.where(inside >= base, 2 * base + other * size + inside - base, place)
        base += size
    return place


def one_hot(place, slot):
    return jnp.where(place == slot, jnp.float32(1.0), jnp.float32(0.0)).astype(jnp.bfloat16)


def store_sums(wave, sizes, live, targets, fetch, chunk_refs):
    rows = targets.shape[1]
    size = sizes[wave]
    place = target_place(targets, sizes)
    place = jnp.where(lax.broadcasted_iota(jnp.int32, (1, rows), 1) < live, place, -1)
    slot = lax.broadcasted_iota(jnp.int32, (size * GROUP, rows), 0) + sum(sizes[:wave]) * GROUP
    chosen = one_hot(place, slot)
    total = fetch(chosen)
    at = 0
    for chunk_ref in chunk_refs:
        count = chunk_ref.shape[0]
        chunk_ref[...] = total[at : at + count]
        at += count


def first_sum_kernel(sizes, live_ref, target_hbm, state_hbm, *refs):
    *chunk_refs, live_out, target_ref, state_ref, sems = refs
    rows = state_ref.shape[0]
    blocks = [pl.ds(first, rows // PARTS) for first in range(0, rows, rows // PARTS)]
    copies = [
        pltpu.make_async_copy(source, place, sems.at[index])
        for index, (source, place) in enumerate(
            [(target_hbm, target_ref)] + [(state_hbm.at[block], state_ref.at[block]) for block in blocks]
        )
    ]
    for copy in copies:
        copy.start()
    live = live_ref[0, 0]
    live_out[...] = jnp.full(live_out.shape, live, jnp.int32)
    copies[0].wait()

    def fetch(chosen):
        total = None
        for index, block in enumerate(blocks):
            copies[1 + index].wait()
            part = slice(index * block.size, (index + 1) * block.size)
            term = jnp.dot(chosen[:, part], state_ref[block, :], preferred_element_type=jnp.float32)
            total = term if total is None else total + term
        return total

    store_sums(0, sizes, live, target_ref[...], fetch, chunk_refs)


def later_sum_kernel(wave, sizes, live_ref, target_ref, state_ref, *chunk_refs):
    def fetch(chosen):
        return jnp.dot(chosen, state_ref[...], preferred_element_type=jnp.float32)

    store_sums(wave, sizes, live_ref[:, :1], target_ref[...], fetch, chunk_refs)


def chunk_shapes(wave, size, channels):
    counts = [size, size, 2 * size] if REDUCE_STEPWISE[wave] else [size] * GROUP
    return [jax.ShapeDtypeStruct((count, channels), jnp.float32) for count in counts]


def first_sums(states, targets, live, sizes):
    rows, channels = states.shape
    handed_on = [
        jax.ShapeDtypeStruct((1, LANES), jnp.int32),
        jax.ShapeDtypeStruct(targets.shape, targets.dtype),
        jax.ShapeDtypeStruct(states.shape, states.dtype),
    ]
    out = call(
        functools.partial(first_sum_kernel, sizes), chunk_shapes(0, sizes[0], channels) + handed_on, [SMEM, HBM, HBM],
        2 * sizes[0] * GROUP * rows * channels,
        [pltpu.SemaphoreType.DMA((1 + PARTS,))],
    )(live, *(pltpu.with_memory_space_constraint(value, pltpu.HBM) for value in (targets, states)))
    return out[:-3], *out[-3:]


def later_sums(states, targets, live, wave, sizes):
    rows, channels = states.shape
    return call(
        functools.partial(later_sum_kernel, wave, sizes), chunk_shapes(wave, sizes[wave], channels), [VMEM] * 3,
        2 * sizes[wave] * GROUP * rows * channels,
    )(live, targets, states)


def choose_kernel(sizes, half, live_ref, target_ref, source_ref, tie_ref, pick_ref, *refs):
    del tie_ref
    rows = target_ref.shape[1]
    sources = source_place(source_ref[...], half)
    for place, part_refs in ((target_place(target_ref[...], sizes), refs[:2]), (sources, refs[2:])):
        place = jnp.transpose(jnp.broadcast_to(place, (LANES, rows)))
        base = 0
        for part_ref in part_refs:
            columns = part_ref.shape[1]
            count = columns // 3
            for first in range(0, columns, LANES):
                width = min(LANES, columns - first)
                slot = (lax.broadcasted_iota(jnp.int32, (1, width), 1) + first) % count + base
                part_ref[:, first : first + width] = one_hot(place[:, :width], slot)
            base += count
    sources = jnp.where(lax.broadcasted_iota(jnp.int32, (1, rows), 1) < live_ref[:, :1], sources, -1)
    pick_ref[...] = one_hot(sources, lax.broadcasted_iota(jnp.int32, pick_ref.shape, 0))


def split_sums(sum_refs, parts_ref):
    total = parts_ref.shape[0] // 3
    value = jnp.concatenate([sum_ref[...] for sum_ref in sum_refs])
    for part in range(3):
        low = value.astype(jnp.bfloat16)
        parts_ref[part * total : (part + 1) * total, :] = low
        value = value - low.astype(jnp.float32)


def gather(chosen_ref, parts_ref):
    return jnp.dot(chosen_ref[...], parts_ref[...], preferred_element_type=jnp.float32)


def gather_kernel(n_sums, *refs):
    sum_refs = refs[:n_sums]
    chosen_ref, state_ref, message_ref, parts_ref = refs[n_sums:]
    split_sums(sum_refs, parts_ref)
    message_ref[...] = gather(chosen_ref, parts_ref) - state_ref[...].astype(jnp.float32)


def gather_first(sums, chosen, states):
    rows, columns = chosen.shape
    channels = sums[0].shape[1]
    return call(
        functools.partial(gather_kernel, len(sums)),
        jax.ShapeDtypeStruct((rows, channels), jnp.float32),
        [VMEM] * (len(sums) + 2), 2 * rows * columns * channels,
        [pltpu.VMEM((columns, channels), jnp.bfloat16)],
    )(*sums, chosen, states)


def normed_activated(message_ref, chosen_ref, parts_ref, inner_ref, gain_ref):
    message = message_ref[...] + gather(chosen_ref, parts_ref)
    mean_square = jnp.mean(message * message, axis=-1, keepdims=True)
    normed = message * lax.rsqrt(mean_square + 1e-05) * gain_ref[...]
    activated = jax.nn.relu(
        jnp.dot(normed.astype(jnp.bfloat16), inner_ref[...], preferred_element_type=jnp.float32)
    ).astype(jnp.bfloat16)
    return normed, activated


def finish(normed, activated, outer_ref):
    return normed + jnp.dot(activated, outer_ref[...], preferred_element_type=jnp.float32)


def only_live(result, live_ref, first_row):
    row = lax.broadcasted_iota(jnp.int32, (result.shape[0], 1), 0) + first_row
    return jnp.where(row < live_ref[:, :1], result, jnp.float32(0.0)).astype(jnp.bfloat16)


def layer_one_kernel(n_sums, *refs):
    sum_refs = refs[:n_sums]
    message_ref, chosen_ref, pick_ref, inner_ref, outer_ref, gain_ref, reverse_ref, *piece_refs, parts_ref = refs[n_sums:]
    split_sums(sum_refs, parts_ref)
    normed, activated = normed_activated(message_ref, chosen_ref, parts_ref, inner_ref, gain_ref)
    reverse_ref[...] = finish(normed, activated, outer_ref).astype(jnp.bfloat16)
    total = jnp.dot(pick_ref[...], reverse_ref[...], preferred_element_type=jnp.float32)
    at = 0
    for piece_ref in piece_refs:
        count = piece_ref.shape[0]
        piece_ref[...] = total[at : at + count]
        at += count


def layer_two_kernel(n_sums, live_ref, *refs):
    sum_refs = refs[:n_sums]
    message_ref, chosen_ref, inner_ref, outer_ref, gain_ref, final_hbm, parts_ref, final_ref, sems = refs[n_sums:]
    split_sums(sum_refs, parts_ref)
    normed, activated = normed_activated(message_ref, chosen_ref, parts_ref, inner_ref, gain_ref)
    block = final_ref.shape[0] // 4
    copies = []
    for index in range(4):
        rows = pl.ds(index * block, block)
        part = slice(index * block, (index + 1) * block)
        final_ref[rows, :] = only_live(
            finish(normed[part], activated[part], outer_ref), live_ref, index * block
        )
        copies.append(pltpu.make_async_copy(final_ref.at[rows], final_hbm.at[rows], sems.at[index]))
        copies[-1].start()
    for copy in copies:
        copy.wait()


def swap(value, axis, mask):
    return lax.ppermute(value, axis, [(i, i ^ mask) for i in range(lax.axis_size(axis))])


def swap_group(value, kind):
    across = lax.axis_size("tgt")
    return lax.ppermute(
        value,
        ("src", "tgt"),
        [
            (i * across + j, (i ^ partner_mask(kind, j % 2)) * across + j)
            for i in range(lax.axis_size("src"))
            for j in range(across)
        ],
    )


def higher_masks(axis, low):
    masks = []
    while low < lax.axis_size(axis):
        masks.append(low)
        low *= 2
    return masks


def tie(value, other):
    return lax.optimization_barrier((value, other))[0]


def spread(total, stepwise):
    if not stepwise:
        return [total] + [swap_group(total, kind) for kind in (NEAR, FAR, BOTH)]
    near = swap_group(total, NEAR)
    return [total, near, swap_group(jnp.concatenate([total, near]), FAR)]


def reduce(chunks, stepwise, ready):
    if not stepwise:
        parts = ready([swap_group(chunks[kind], kind) for kind in (BOTH, NEAR, FAR)])
        return chunks[0] + parts[0] + parts[1] + parts[2]
    size = chunks[0].shape[0]
    part = swap_group(chunks[2], FAR)
    return chunks[0] + part[:size] + ready(swap_group(chunks[1] + part[size:], NEAR))


def target_totals(waves, between):
    first = reduce(waves[0], REDUCE_STEPWISE[0], lambda parts: parts)
    made = between(first)
    second = reduce(waves[1], REDUCE_STEPWISE[1], lambda parts: tie(parts, made))
    sums = [first, second]
    for mask in higher_masks("src", GROUP):
        parts = [swap(value, "src", mask) for value in sums]
        first = sums[0] + tie(parts[0], sums[1])
        sums = [first, sums[1] + parts[1]]
    return [spread(value, stepwise) for value, stepwise in zip(sums, SPREAD_STEPWISE)], made


def source_totals(pieces):
    own = [mine + swap(theirs, "tgt", 1) for mine, theirs in pieces]
    for mask in higher_masks("tgt", 2):
        own = [value + swap(value, "tgt", mask) for value in own]
    return [[value, swap(value, "tgt", 1)] for value in own]


def body(
    edge_state,
    edge_source,
    edge_target,
    live_edges,
    inner_one,
    outer_one,
    inner_two,
    outer_two,
    gain_one,
    gain_two,
):
    rows, channels = edge_state.shape[2:]
    states = edge_state.reshape(rows, channels)
    sources = edge_source.reshape(1, rows)
    targets = edge_target.reshape(1, rows)
    target_atoms = ATOM_DEV * lax.axis_size("src")
    source_atoms = ATOM_DEV * lax.axis_size("tgt")
    sizes = wave_sizes(target_atoms)
    half = source_atoms // 2
    first, live, targets, states = first_sums(states, targets, live_edges, sizes)
    waves = [first] + [later_sums(states, targets, live, wave, sizes) for wave in range(1, len(sizes))]

    pieces = piece_sizes(half)
    parts = (
        GROUP * sizes[0] + sizes[1], (GROUP - 1) * sizes[1], 2 * pieces[0] + pieces[1], pieces[1]
    )

    def choose(first):
        return call(
            functools.partial(choose_kernel, sizes, half),
            [jax.ShapeDtypeStruct((source_atoms, rows), jnp.bfloat16)]
            + [jax.ShapeDtypeStruct((rows, 3 * count), jnp.bfloat16) for count in parts],
            [VMEM] * 4, HIDE_FLOPS,
        )(live, targets, sources, first)

    totals, (source_pick, *chosen) = target_totals(waves, choose)
    early, late = totals[0] + totals[1][:1], totals[1][1:]
    message = gather_first(early, chosen[0], states)
    reverse_state, *sums = call(
        functools.partial(layer_one_kernel, len(late)),
        [jax.ShapeDtypeStruct((rows, channels), jnp.bfloat16)]
        + [jax.ShapeDtypeStruct((size, channels), jnp.float32) for size in pieces for _ in range(2)],
        [VMEM] * (len(late) + 6),
        2 * rows * channels * (3 * parts[1] + 2 * channels + source_atoms),
        [pltpu.VMEM((3 * parts[1], channels), jnp.bfloat16)],
    )(*late, message, chosen[1], source_pick, inner_one, outer_one, gain_one.reshape(1, channels))
    totals = source_totals(list(zip(sums[::2], sums[1::2])))
    early, late = totals[0] + totals[1][:1], totals[1][1:]
    message = gather_first(early, chosen[2], reverse_state)
    final_state = call(
        functools.partial(layer_two_kernel, len(late)),
        jax.ShapeDtypeStruct((rows, channels), jnp.bfloat16),
        [VMEM] * (len(late) + 6),
        2 * rows * channels * (3 * parts[3] + 2 * channels),
        [
            pltpu.VMEM((3 * parts[3], channels), jnp.bfloat16),
            pltpu.VMEM((rows, channels), jnp.bfloat16),
            pltpu.SemaphoreType.DMA((4,)),
        ],
        HBM,
    )(live, *late, message, chosen[3], inner_two, outer_two, gain_two.reshape(1, channels))
    return final_state.reshape(1, 1, rows, channels)


def solution(mesh):
    placed = (
        P("src", "tgt", None, None),
        P("src", "tgt", None),
        P("src", "tgt", None),
        P("src", "tgt"),
        P(),
        P(),
        P(),
        P(),
        P(),
        P(),
    )
    return jax.shard_map(
        body, mesh=mesh, in_specs=placed, out_specs=P("src", "tgt", None, None), check_vma=False
    )
```

```python
import functools

import jax
import jax.numpy as jnp
from jax import lax
from jax.experimental import pallas as pl
from jax.experimental.pallas import tpu as pltpu
from jax.sharding import PartitionSpec as P

ATOM_DEV = 64
GROUP = 4
NEAR, FAR, BOTH = 1, 2, 3
SHARES = (4, 4)
REDUCE_STEPWISE = (False, True)
SPREAD_STEPWISE = (False, False)
PIECES = (1, 1)
PARTS = 4
LANES = 128
HIDE_FLOPS = 8 * 10**9
VMEM_LIMIT = 40 * 1024 * 1024

VMEM = pl.BlockSpec(memory_space=pltpu.VMEM)
HBM = pl.BlockSpec(memory_space=pltpu.HBM)
SMEM = pl.BlockSpec(memory_space=pltpu.SMEM)


def call(kernel, out_shape, in_specs, flops, scratch=(), out_specs=None):
    return pl.pallas_call(
        kernel,
        out_shape=out_shape,
        in_specs=in_specs,
        out_specs=jax.tree.map(lambda _: VMEM, out_shape) if out_specs is None else out_specs,
        scratch_shapes=list(scratch),
        compiler_params=pltpu.CompilerParams(vmem_limit_bytes=VMEM_LIMIT),
        cost_estimate=pl.CostEstimate(flops=flops, bytes_accessed=0, transcendentals=0),
    )


def wave_sizes(atoms):
    return [atoms // (GROUP * sum(SHARES)) * share for share in SHARES]


def partner_mask(kind, core):
    if kind in (NEAR, FAR) and core == 0:
        return NEAR + FAR - kind
    return kind


def target_place(atoms, sizes):
    device = lax.axis_index("src")
    low, high = device % 2, (device // 2) % 2
    own = jnp.where(lax.axis_index("tgt") % 2 == 0, high + 2 * low, low + 2 * high)
    place = atoms
    base = 0
    for size in sizes:
        inside = atoms - base
        chunk = sum((inside >= k * size).astype(jnp.int32) for k in range(1, GROUP))
        spot = base + jnp.bitwise_xor(chunk, own) * size + inside - chunk * size
        place = jnp.where(inside >= 0, spot, place)
        base += GROUP * size
    return place


def piece_sizes(half):
    return [half // sum(PIECES) * piece for piece in PIECES]


def source_place(atoms, half):
    own = (lax.axis_index("tgt") % 2) * half
    ours = jnp.bitwise_xor(atoms, own)
    other = (ours >= half).astype(jnp.int32)
    inside = ours - other * half
    place = atoms
    base = 0
    for size in piece_sizes(half):
        place = jnp.where(inside >= base, 2 * base + other * size + inside - base, place)
        base += size
    return place


def one_hot(place, slot):
    return jnp.where(place == slot, jnp.float32(1.0), jnp.float32(0.0)).astype(jnp.bfloat16)


def store_sums(wave, sizes, live, targets, fetch, chunk_refs, first_chunk=0):
    rows = targets.shape[1]
    size = sizes[wave]
    place = target_place(targets, sizes)
    place = jnp.where(lax.broadcasted_iota(jnp.int32, (1, rows), 1) < live, place, -1)
    count = sum(chunk_ref.shape[0] for chunk_ref in chunk_refs)
    base = sum(sizes[:wave]) * GROUP + first_chunk * size
    slot = lax.broadcasted_iota(jnp.int32, (count, rows), 0) + base
    chosen = one_hot(place, slot)
    total = fetch(chosen)
    at = 0
    for chunk_ref in chunk_refs:
        count = chunk_ref.shape[0]
        chunk_ref[...] = total[at : at + count]
        at += count


def first_sum_kernel(sizes, live_ref, target_hbm, state_hbm, *refs):
    *chunk_refs, live_out, target_ref, state_ref, sems = refs
    rows = state_ref.shape[0]
    blocks = [pl.ds(first, rows // PARTS) for first in range(0, rows, rows // PARTS)]
    copies = [
        pltpu.make_async_copy(source, place, sems.at[index])
        for index, (source, place) in enumerate(
            [(target_hbm, target_ref)] + [(state_hbm.at[block], state_ref.at[block]) for block in blocks]
        )
    ]
    for copy in copies:
        copy.start()
    live = live_ref[0, 0]
    live_out[...] = jnp.full(live_out.shape, live, jnp.int32)
    copies[0].wait()

    def fetch(chosen):
        total = None
        for index, block in enumerate(blocks):
            copies[1 + index].wait()
            part = slice(index * block.size, (index + 1) * block.size)
            term = jnp.dot(chosen[:, part], state_ref[block, :], preferred_element_type=jnp.float32)
            total = term if total is None else total + term
        return total

    store_sums(0, sizes, live, target_ref[...], fetch, chunk_refs, BOTH)


def later_sum_kernel(wave, sizes, live_ref, target_ref, state_ref, *chunk_refs):
    def fetch(chosen):
        return jnp.dot(chosen, state_ref[...], preferred_element_type=jnp.float32)

    store_sums(wave, sizes, live_ref[:, :1], target_ref[...], fetch, chunk_refs)


def chunk_shapes(wave, size, channels):
    counts = [size, size, 2 * size] if REDUCE_STEPWISE[wave] else [size] * GROUP
    return [jax.ShapeDtypeStruct((count, channels), jnp.float32) for count in counts]


def first_sums(states, targets, live, sizes):
    rows, channels = states.shape
    handed_on = [
        jax.ShapeDtypeStruct((1, LANES), jnp.int32),
        jax.ShapeDtypeStruct(targets.shape, targets.dtype),
        jax.ShapeDtypeStruct(states.shape, states.dtype),
    ]
    out = call(
        functools.partial(first_sum_kernel, sizes), chunk_shapes(0, sizes[0], channels)[BOTH:] + handed_on, [SMEM, HBM, HBM],
        2 * sizes[0] * rows * channels,
        [pltpu.SemaphoreType.DMA((1 + PARTS,))],
    )(live, *(pltpu.with_memory_space_constraint(value, pltpu.HBM) for value in (targets, states)))
    return out[:-3], *out[-3:]


def later_sums(states, targets, live, wave, sizes, shapes, flops):
    return call(
        functools.partial(later_sum_kernel, wave, sizes), shapes, [VMEM] * 3, flops,
    )(live, targets, states)


def choose_kernel(sizes, half, live_ref, target_ref, source_ref, tie_ref, pick_ref, *refs):
    del tie_ref
    rows = target_ref.shape[1]
    sources = source_place(source_ref[...], half)
    for place, part_refs in ((target_place(target_ref[...], sizes), refs[:2]), (sources, refs[2:])):
        place = jnp.transpose(jnp.broadcast_to(place, (LANES, rows)))
        base = 0
        for part_ref in part_refs:
            columns = part_ref.shape[1]
            count = columns // 3
            for first in range(0, columns, LANES):
                width = min(LANES, columns - first)
                slot = (lax.broadcasted_iota(jnp.int32, (1, width), 1) + first) % count + base
                part_ref[:, first : first + width] = one_hot(place[:, :width], slot)
            base += count
    sources = jnp.where(lax.broadcasted_iota(jnp.int32, (1, rows), 1) < live_ref[:, :1], sources, -1)
    pick_ref[...] = one_hot(sources, lax.broadcasted_iota(jnp.int32, pick_ref.shape, 0))


def split_sums(sum_refs, parts_ref):
    total = parts_ref.shape[0] // 3
    value = jnp.concatenate([sum_ref[...] for sum_ref in sum_refs])
    for part in range(3):
        low = value.astype(jnp.bfloat16)
        parts_ref[part * total : (part + 1) * total, :] = low
        value = value - low.astype(jnp.float32)


def gather(chosen_ref, parts_ref):
    return jnp.dot(chosen_ref[...], parts_ref[...], preferred_element_type=jnp.float32)


def gather_kernel(n_sums, *refs):
    sum_refs = refs[:n_sums]
    chosen_ref, state_ref, message_ref, parts_ref = refs[n_sums:]
    split_sums(sum_refs, parts_ref)
    message_ref[...] = gather(chosen_ref, parts_ref) - state_ref[...].astype(jnp.float32)


def gather_first(sums, chosen, states):
    rows, columns = chosen.shape
    channels = sums[0].shape[1]
    return call(
        functools.partial(gather_kernel, len(sums)),
        jax.ShapeDtypeStruct((rows, channels), jnp.float32),
        [VMEM] * (len(sums) + 2), 2 * rows * columns * channels,
        [pltpu.VMEM((columns, channels), jnp.bfloat16)],
    )(*sums, chosen, states)


def normed_activated(message_ref, chosen_ref, parts_ref, inner_ref, gain_ref):
    message = message_ref[...] + gather(chosen_ref, parts_ref)
    mean_square = jnp.mean(message * message, axis=-1, keepdims=True)
    normed = message * lax.rsqrt(mean_square + 1e-05) * gain_ref[...]
    activated = jax.nn.relu(
        jnp.dot(normed.astype(jnp.bfloat16), inner_ref[...], preferred_element_type=jnp.float32)
    ).astype(jnp.bfloat16)
    return normed, activated


def finish(normed, activated, outer_ref):
    return normed + jnp.dot(activated, outer_ref[...], preferred_element_type=jnp.float32)


def only_live(result, live_ref, first_row):
    row = lax.broadcasted_iota(jnp.int32, (result.shape[0], 1), 0) + first_row
    return jnp.where(row < live_ref[:, :1], result, jnp.float32(0.0)).astype(jnp.bfloat16)


def layer_one_kernel(n_sums, *refs):
    sum_refs = refs[:n_sums]
    message_ref, chosen_ref, pick_ref, inner_ref, outer_ref, gain_ref, reverse_ref, *piece_refs, parts_ref = refs[n_sums:]
    split_sums(sum_refs, parts_ref)
    normed, activated = normed_activated(message_ref, chosen_ref, parts_ref, inner_ref, gain_ref)
    reverse_ref[...] = finish(normed, activated, outer_ref).astype(jnp.bfloat16)
    total = jnp.dot(pick_ref[...], reverse_ref[...], preferred_element_type=jnp.float32)
    at = 0
    for piece_ref in piece_refs:
        count = piece_ref.shape[0]
        piece_ref[...] = total[at : at + count]
        at += count


def layer_two_kernel(n_sums, live_ref, *refs):
    sum_refs = refs[:n_sums]
    message_ref, chosen_ref, inner_ref, outer_ref, gain_ref, final_hbm, parts_ref, final_ref, sems = refs[n_sums:]
    split_sums(sum_refs, parts_ref)
    normed, activated = normed_activated(message_ref, chosen_ref, parts_ref, inner_ref, gain_ref)
    block = final_ref.shape[0] // 4
    copies = []
    for index in range(4):
        rows = pl.ds(index * block, block)
        part = slice(index * block, (index + 1) * block)
        final_ref[rows, :] = only_live(
            finish(normed[part], activated[part], outer_ref), live_ref, index * block
        )
        copies.append(pltpu.make_async_copy(final_ref.at[rows], final_hbm.at[rows], sems.at[index]))
        copies[-1].start()
    for copy in copies:
        copy.wait()


def swap(value, axis, mask):
    return lax.ppermute(value, axis, [(i, i ^ mask) for i in range(lax.axis_size(axis))])


def swap_group(value, kind):
    across = lax.axis_size("tgt")
    return lax.ppermute(
        value,
        ("src", "tgt"),
        [
            (i * across + j, (i ^ partner_mask(kind, j % 2)) * across + j)
            for i in range(lax.axis_size("src"))
            for j in range(across)
        ],
    )


def higher_masks(axis, low):
    masks = []
    while low < lax.axis_size(axis):
        masks.append(low)
        low *= 2
    return masks


def tie(value, other):
    return lax.optimization_barrier((value, other))[0]


def spread(total, stepwise):
    if not stepwise:
        return [total] + [swap_group(total, kind) for kind in (NEAR, FAR, BOTH)]
    near = swap_group(total, NEAR)
    return [total, near, swap_group(jnp.concatenate([total, near]), FAR)]


def reduce(chunks, stepwise, ready):
    if not stepwise:
        parts = ready([swap_group(chunks[kind], kind) for kind in (BOTH, NEAR, FAR)])
        return chunks[0] + parts[0] + parts[1] + parts[2]
    size = chunks[0].shape[0]
    part = swap_group(chunks[2], FAR)
    return chunks[0] + part[:size] + ready(swap_group(chunks[1] + part[size:], NEAR))


def target_totals(waves, between):
    first = reduce(waves[0], REDUCE_STEPWISE[0], lambda parts: parts)
    made = between(first)
    second = reduce(waves[1], REDUCE_STEPWISE[1], lambda parts: tie(parts, made))
    sums = [first, second]
    for mask in higher_masks("src", GROUP):
        parts = [swap(value, "src", mask) for value in sums]
        first = sums[0] + tie(parts[0], sums[1])
        sums = [first, sums[1] + tie(parts[1], first)]
    return [spread(value, stepwise) for value, stepwise in zip(sums, SPREAD_STEPWISE)], made


def source_totals(pieces):
    own = [mine + swap(theirs, "tgt", 1) for mine, theirs in pieces]
    for mask in higher_masks("tgt", 2):
        own = [value + swap(value, "tgt", mask) for value in own]
    return [[value, swap(value, "tgt", 1)] for value in own]


def body(
    edge_state,
    edge_source,
    edge_target,
    live_edges,
    inner_one,
    outer_one,
    inner_two,
    outer_two,
    gain_one,
    gain_two,
):
    rows, channels = edge_state.shape[2:]
    states = edge_state.reshape(rows, channels)
    sources = edge_source.reshape(1, rows)
    targets = edge_target.reshape(1, rows)
    target_atoms = ATOM_DEV * lax.axis_size("src")
    source_atoms = ATOM_DEV * lax.axis_size("tgt")
    sizes = wave_sizes(target_atoms)
    half = source_atoms // 2
    first, live, targets, states = first_sums(states, targets, live_edges, sizes)
    shapes = [chunk_shapes(wave, size, channels) for wave, size in enumerate(sizes)]
    rest = later_sums(states, targets, live, 0, sizes, shapes[0][:BOTH], 2 * BOTH * sizes[0] * rows * channels)
    waves = [rest + first, later_sums(states, targets, live, 1, sizes, shapes[1], 2 * GROUP * sizes[1] * rows * channels)]

    pieces = piece_sizes(half)
    parts = (
        GROUP * sizes[0] + sizes[1], (GROUP - 1) * sizes[1], 2 * pieces[0] + pieces[1], pieces[1]
    )

    def choose(first):
        return call(
            functools.partial(choose_kernel, sizes, half),
            [jax.ShapeDtypeStruct((source_atoms, rows), jnp.bfloat16)]
            + [jax.ShapeDtypeStruct((rows, 3 * count), jnp.bfloat16) for count in parts],
            [VMEM] * 4, HIDE_FLOPS,
        )(live, targets, sources, first)

    totals, (source_pick, *chosen) = target_totals(waves, choose)
    early, late = totals[0] + totals[1][:1], totals[1][1:]
    message = gather_first(early, chosen[0], states)
    reverse_state, *sums = call(
        functools.partial(layer_one_kernel, len(late)),
        [jax.ShapeDtypeStruct((rows, channels), jnp.bfloat16)]
        + [jax.ShapeDtypeStruct((size, channels), jnp.float32) for size in pieces for _ in range(2)],
        [VMEM] * (len(late) + 6),
        2 * rows * channels * (3 * parts[1] + 2 * channels + source_atoms),
        [pltpu.VMEM((3 * parts[1], channels), jnp.bfloat16)],
    )(*late, message, chosen[1], source_pick, inner_one, outer_one, gain_one.reshape(1, channels))
    totals = source_totals(list(zip(sums[::2], sums[1::2])))
    early, late = totals[0] + totals[1][:1], totals[1][1:]
    message = gather_first(early, chosen[2], reverse_state)
    final_state = call(
        functools.partial(layer_two_kernel, len(late)),
        jax.ShapeDtypeStruct((rows, channels), jnp.bfloat16),
        [VMEM] * (len(late) + 6),
        2 * rows * channels * (3 * parts[3] + 2 * channels),
        [
            pltpu.VMEM((3 * parts[3], channels), jnp.bfloat16),
            pltpu.VMEM((rows, channels), jnp.bfloat16),
            pltpu.SemaphoreType.DMA((4,)),
        ],
        HBM,
    )(live, *late, message, chosen[3], inner_two, outer_two, gain_two.reshape(1, channels))
    return final_state.reshape(1, 1, rows, channels)


def solution(mesh):
    placed = (
        P("src", "tgt", None, None),
        P("src", "tgt", None),
        P("src", "tgt", None),
        P("src", "tgt"),
        P(),
        P(),
        P(),
        P(),
        P(),
        P(),
    )
    return jax.shard_map(
        body, mesh=mesh, in_specs=placed, out_specs=P("src", "tgt", None, None), check_vma=False
    )
```

```python
import functools

import jax
import jax.numpy as jnp
from jax import lax
from jax.experimental import pallas as pl
from jax.experimental.pallas import tpu as pltpu
from jax.sharding import PartitionSpec as P

ATOM_DEV = 64
GROUP = 4
NEAR, FAR, BOTH = 1, 2, 3
SHARES = (4, 4)
REDUCE_STEPWISE = (False, True)
SPREAD_STEPWISE = (False, False)
PIECES = (1, 1)
PARTS = 4
LANES = 128
HIDE_FLOPS = 8 * 10**9
VMEM_LIMIT = 40 * 1024 * 1024

VMEM = pl.BlockSpec(memory_space=pltpu.VMEM)
HBM = pl.BlockSpec(memory_space=pltpu.HBM)
SMEM = pl.BlockSpec(memory_space=pltpu.SMEM)


def call(kernel, out_shape, in_specs, flops, scratch=(), out_specs=None):
    return pl.pallas_call(
        kernel,
        out_shape=out_shape,
        in_specs=in_specs,
        out_specs=jax.tree.map(lambda _: VMEM, out_shape) if out_specs is None else out_specs,
        scratch_shapes=list(scratch),
        compiler_params=pltpu.CompilerParams(vmem_limit_bytes=VMEM_LIMIT),
        cost_estimate=pl.CostEstimate(flops=flops, bytes_accessed=0, transcendentals=0),
    )


def wave_sizes(atoms):
    return [atoms // (GROUP * sum(SHARES)) * share for share in SHARES]


def partner_mask(kind, core):
    if kind in (NEAR, FAR) and core == 0:
        return NEAR + FAR - kind
    return kind


def target_place(atoms, sizes):
    device = lax.axis_index("src")
    low, high = device % 2, (device // 2) % 2
    own = jnp.where(lax.axis_index("tgt") % 2 == 0, high + 2 * low, low + 2 * high)
    place = atoms
    base = 0
    for size in sizes:
        inside = atoms - base
        chunk = sum((inside >= k * size).astype(jnp.int32) for k in range(1, GROUP))
        spot = base + jnp.bitwise_xor(chunk, own) * size + inside - chunk * size
        place = jnp.where(inside >= 0, spot, place)
        base += GROUP * size
    return place


def piece_sizes(half):
    return [half // sum(PIECES) * piece for piece in PIECES]


def source_place(atoms, half):
    own = (lax.axis_index("tgt") % 2) * half
    ours = jnp.bitwise_xor(atoms, own)
    other = (ours >= half).astype(jnp.int32)
    inside = ours - other * half
    place = atoms
    base = 0
    for size in piece_sizes(half):
        place = jnp.where(inside >= base, 2 * base + other * size + inside - base, place)
        base += size
    return place


def one_hot(place, slot):
    return jnp.where(place == slot, jnp.float32(1.0), jnp.float32(0.0)).astype(jnp.bfloat16)


def store_sums(wave, sizes, live, targets, fetch, chunk_refs, first_chunk=0):
    rows = targets.shape[1]
    size = sizes[wave]
    place = target_place(targets, sizes)
    place = jnp.where(lax.broadcasted_iota(jnp.int32, (1, rows), 1) < live, place, -1)
    count = sum(chunk_ref.shape[0] for chunk_ref in chunk_refs)
    slot = lax.broadcasted_iota(jnp.int32, (count, rows), 0) + sum(sizes[:wave]) * GROUP + first_chunk * size
    chosen = one_hot(place, slot)
    total = fetch(chosen)
    at = 0
    for chunk_ref in chunk_refs:
        count = chunk_ref.shape[0]
        chunk_ref[...] = total[at : at + count]
        at += count


def first_sum_kernel(sizes, live_ref, target_hbm, state_hbm, *refs):
    *chunk_refs, live_out, target_ref, state_ref, sems = refs
    rows = state_ref.shape[0]
    blocks = [pl.ds(first, rows // PARTS) for first in range(0, rows, rows // PARTS)]
    copies = [
        pltpu.make_async_copy(source, place, sems.at[index])
        for index, (source, place) in enumerate(
            [(target_hbm, target_ref)] + [(state_hbm.at[block], state_ref.at[block]) for block in blocks]
        )
    ]
    for copy in copies:
        copy.start()
    live = live_ref[0, 0]
    live_out[...] = jnp.full(live_out.shape, live, jnp.int32)
    copies[0].wait()

    def fetch(chosen):
        total = None
        for index, block in enumerate(blocks):
            copies[1 + index].wait()
            part = slice(index * block.size, (index + 1) * block.size)
            term = jnp.dot(chosen[:, part], state_ref[block, :], preferred_element_type=jnp.float32)
            total = term if total is None else total + term
        return total

    store_sums(0, sizes, live, target_ref[...], fetch, chunk_refs)


def later_sum_kernel(wave, sizes, first_chunk, live_ref, target_ref, state_ref, *chunk_refs):
    def fetch(chosen):
        return jnp.dot(chosen, state_ref[...], preferred_element_type=jnp.float32)

    store_sums(wave, sizes, live_ref[:, :1], target_ref[...], fetch, chunk_refs, first_chunk)


def chunk_shapes(wave, size, channels):
    counts = [size, size, 2 * size] if REDUCE_STEPWISE[wave] else [size] * GROUP
    return [jax.ShapeDtypeStruct((count, channels), jnp.float32) for count in counts]


def first_sums(states, targets, live, sizes):
    rows, channels = states.shape
    handed_on = [
        jax.ShapeDtypeStruct((1, LANES), jnp.int32),
        jax.ShapeDtypeStruct(targets.shape, targets.dtype),
        jax.ShapeDtypeStruct(states.shape, states.dtype),
    ]
    out = call(
        functools.partial(first_sum_kernel, sizes), chunk_shapes(0, sizes[0], channels) + handed_on, [SMEM, HBM, HBM],
        2 * sizes[0] * GROUP * rows * channels,
        [pltpu.SemaphoreType.DMA((1 + PARTS,))],
    )(live, *(pltpu.with_memory_space_constraint(value, pltpu.HBM) for value in (targets, states)))
    return out[:-3], *out[-3:]


def later_sums(states, targets, live, wave, sizes):
    rows, channels = states.shape
    shapes = chunk_shapes(wave, sizes[wave], channels)

    def some(first_chunk, chosen_shapes):
        return call(
            functools.partial(later_sum_kernel, wave, sizes, first_chunk), chosen_shapes, [VMEM] * 3,
            sizes[wave] * GROUP * rows * channels,
        )(live, targets, states)

    sent = some(2, shapes[2:])
    return some(0, shapes[:2]) + sent


def choose_kernel(sizes, half, live_ref, target_ref, source_ref, tie_ref, pick_ref, *refs):
    del tie_ref
    rows = target_ref.shape[1]
    sources = source_place(source_ref[...], half)
    for place, part_refs in ((target_place(target_ref[...], sizes), refs[:2]), (sources, refs[2:])):
        place = jnp.transpose(jnp.broadcast_to(place, (LANES, rows)))
        base = 0
        for part_ref in part_refs:
            columns = part_ref.shape[1]
            count = columns // 3
            for first in range(0, columns, LANES):
                width = min(LANES, columns - first)
                slot = (lax.broadcasted_iota(jnp.int32, (1, width), 1) + first) % count + base
                part_ref[:, first : first + width] = one_hot(place[:, :width], slot)
            base += count
    sources = jnp.where(lax.broadcasted_iota(jnp.int32, (1, rows), 1) < live_ref[:, :1], sources, -1)
    pick_ref[...] = one_hot(sources, lax.broadcasted_iota(jnp.int32, pick_ref.shape, 0))


def split_sums(sum_refs, parts_ref):
    total = parts_ref.shape[0] // 3
    value = jnp.concatenate([sum_ref[...] for sum_ref in sum_refs])
    for part in range(3):
        low = value.astype(jnp.bfloat16)
        parts_ref[part * total : (part + 1) * total, :] = low
        value = value - low.astype(jnp.float32)


def gather(chosen_ref, parts_ref):
    return jnp.dot(chosen_ref[...], parts_ref[...], preferred_element_type=jnp.float32)


def gather_kernel(n_sums, *refs):
    sum_refs = refs[:n_sums]
    chosen_ref, state_ref, message_ref, parts_ref = refs[n_sums:]
    split_sums(sum_refs, parts_ref)
    message_ref[...] = gather(chosen_ref, parts_ref) - state_ref[...].astype(jnp.float32)


def gather_first(sums, chosen, states):
    rows, columns = chosen.shape
    channels = sums[0].shape[1]
    return call(
        functools.partial(gather_kernel, len(sums)),
        jax.ShapeDtypeStruct((rows, channels), jnp.float32),
        [VMEM] * (len(sums) + 2), 2 * rows * columns * channels,
        [pltpu.VMEM((columns, channels), jnp.bfloat16)],
    )(*sums, chosen, states)


def normed_activated(message_ref, chosen_ref, parts_ref, inner_ref, gain_ref):
    message = message_ref[...] + gather(chosen_ref, parts_ref)
    mean_square = jnp.mean(message * message, axis=-1, keepdims=True)
    normed = message * lax.rsqrt(mean_square + 1e-05) * gain_ref[...]
    activated = jax.nn.relu(
        jnp.dot(normed.astype(jnp.bfloat16), inner_ref[...], preferred_element_type=jnp.float32)
    ).astype(jnp.bfloat16)
    return normed, activated


def finish(normed, activated, outer_ref):
    return normed + jnp.dot(activated, outer_ref[...], preferred_element_type=jnp.float32)


def only_live(result, live_ref, first_row):
    row = lax.broadcasted_iota(jnp.int32, (result.shape[0], 1), 0) + first_row
    return jnp.where(row < live_ref[:, :1], result, jnp.float32(0.0)).astype(jnp.bfloat16)


def layer_one_kernel(n_sums, *refs):
    sum_refs = refs[:n_sums]
    message_ref, chosen_ref, pick_ref, inner_ref, outer_ref, gain_ref, reverse_ref, *piece_refs, parts_ref = refs[n_sums:]
    split_sums(sum_refs, parts_ref)
    normed, activated = normed_activated(message_ref, chosen_ref, parts_ref, inner_ref, gain_ref)
    reverse_ref[...] = finish(normed, activated, outer_ref).astype(jnp.bfloat16)
    total = jnp.dot(pick_ref[...], reverse_ref[...], preferred_element_type=jnp.float32)
    at = 0
    for piece_ref in piece_refs:
        count = piece_ref.shape[0]
        piece_ref[...] = total[at : at + count]
        at += count


def layer_two_kernel(n_sums, live_ref, *refs):
    sum_refs = refs[:n_sums]
    message_ref, chosen_ref, inner_ref, outer_ref, gain_ref, final_hbm, parts_ref, final_ref, sems = refs[n_sums:]
    split_sums(sum_refs, parts_ref)
    normed, activated = normed_activated(message_ref, chosen_ref, parts_ref, inner_ref, gain_ref)
    block = final_ref.shape[0] // 4
    copies = []
    for index in range(4):
        rows = pl.ds(index * block, block)
        part = slice(index * block, (index + 1) * block)
        final_ref[rows, :] = only_live(
            finish(normed[part], activated[part], outer_ref), live_ref, index * block
        )
        copies.append(pltpu.make_async_copy(final_ref.at[rows], final_hbm.at[rows], sems.at[index]))
        copies[-1].start()
    for copy in copies:
        copy.wait()


def swap(value, axis, mask):
    return lax.ppermute(value, axis, [(i, i ^ mask) for i in range(lax.axis_size(axis))])


def swap_group(value, kind):
    across = lax.axis_size("tgt")
    return lax.ppermute(
        value,
        ("src", "tgt"),
        [
            (i * across + j, (i ^ partner_mask(kind, j % 2)) * across + j)
            for i in range(lax.axis_size("src"))
            for j in range(across)
        ],
    )


def higher_masks(axis, low):
    masks = []
    while low < lax.axis_size(axis):
        masks.append(low)
        low *= 2
    return masks


def tie(value, other):
    return lax.optimization_barrier((value, other))[0]


def spread(total, stepwise):
    if not stepwise:
        return [total] + [swap_group(total, kind) for kind in (NEAR, FAR, BOTH)]
    near = swap_group(total, NEAR)
    return [total, near, swap_group(jnp.concatenate([total, near]), FAR)]


def reduce(chunks, stepwise, ready):
    if not stepwise:
        parts = ready([swap_group(chunks[kind], kind) for kind in (BOTH, NEAR, FAR)])
        return chunks[0] + parts[0] + parts[1] + parts[2]
    size = chunks[0].shape[0]
    part = swap_group(chunks[2], FAR)
    return chunks[0] + part[:size] + ready(swap_group(chunks[1] + part[size:], NEAR))


def target_totals(waves, between):
    first = reduce(waves[0], REDUCE_STEPWISE[0], lambda parts: parts)
    made = between(first)
    second = reduce(waves[1], REDUCE_STEPWISE[1], lambda parts: tie(parts, made))
    sums = [first, second]
    for mask in higher_masks("src", GROUP):
        parts = [swap(value, "src", mask) for value in sums]
        first = sums[0] + tie(parts[0], sums[1])
        sums = [first, sums[1] + tie(parts[1], first)]
    return [spread(value, stepwise) for value, stepwise in zip(sums, SPREAD_STEPWISE)], made


def source_totals(pieces):
    own = [mine + swap(theirs, "tgt", 1) for mine, theirs in pieces]
    for mask in higher_masks("tgt", 2):
        own = [value + swap(value, "tgt", mask) for value in own]
    return [[value, swap(value, "tgt", 1)] for value in own]


def body(
    edge_state,
    edge_source,
    edge_target,
    live_edges,
    inner_one,
    outer_one,
    inner_two,
    outer_two,
    gain_one,
    gain_two,
):
    rows, channels = edge_state.shape[2:]
    states = edge_state.reshape(rows, channels)
    sources = edge_source.reshape(1, rows)
    targets = edge_target.reshape(1, rows)
    target_atoms = ATOM_DEV * lax.axis_size("src")
    source_atoms = ATOM_DEV * lax.axis_size("tgt")
    sizes = wave_sizes(target_atoms)
    half = source_atoms // 2
    first, live, targets, states = first_sums(states, targets, live_edges, sizes)
    waves = [first] + [later_sums(states, targets, live, wave, sizes) for wave in range(1, len(sizes))]

    pieces = piece_sizes(half)
    parts = (
        GROUP * sizes[0] + sizes[1], (GROUP - 1) * sizes[1], 2 * pieces[0] + pieces[1], pieces[1]
    )

    def choose(first):
        return call(
            functools.partial(choose_kernel, sizes, half),
            [jax.ShapeDtypeStruct((source_atoms, rows), jnp.bfloat16)]
            + [jax.ShapeDtypeStruct((rows, 3 * count), jnp.bfloat16) for count in parts],
            [VMEM] * 4, HIDE_FLOPS,
        )(live, targets, sources, first)

    totals, (source_pick, *chosen) = target_totals(waves, choose)
    early, late = totals[0] + totals[1][:1], totals[1][1:]
    message = gather_first(early, chosen[0], states)
    reverse_state, *sums = call(
        functools.partial(layer_one_kernel, len(late)),
        [jax.ShapeDtypeStruct((rows, channels), jnp.bfloat16)]
        + [jax.ShapeDtypeStruct((size, channels), jnp.float32) for size in pieces for _ in range(2)],
        [VMEM] * (len(late) + 6),
        2 * rows * channels * (3 * parts[1] + 2 * channels + source_atoms),
        [pltpu.VMEM((3 * parts[1], channels), jnp.bfloat16)],
    )(*late, message, chosen[1], source_pick, inner_one, outer_one, gain_one.reshape(1, channels))
    totals = source_totals(list(zip(sums[::2], sums[1::2])))
    early, late = totals[0] + totals[1][:1], totals[1][1:]
    message = gather_first(early, chosen[2], reverse_state)
    final_state = call(
        functools.partial(layer_two_kernel, len(late)),
        jax.ShapeDtypeStruct((rows, channels), jnp.bfloat16),
        [VMEM] * (len(late) + 6),
        2 * rows * channels * (3 * parts[3] + 2 * channels),
        [
            pltpu.VMEM((3 * parts[3], channels), jnp.bfloat16),
            pltpu.VMEM((rows, channels), jnp.bfloat16),
            pltpu.SemaphoreType.DMA((4,)),
        ],
        HBM,
    )(live, *late, message, chosen[3], inner_two, outer_two, gain_two.reshape(1, channels))
    return final_state.reshape(1, 1, rows, channels)


def solution(mesh):
    placed = (
        P("src", "tgt", None, None),
        P("src", "tgt", None),
        P("src", "tgt", None),
        P("src", "tgt"),
        P(),
        P(),
        P(),
        P(),
        P(),
        P(),
    )
    return jax.shard_map(
        body, mesh=mesh, in_specs=placed, out_specs=P("src", "tgt", None, None), check_vma=False
    )
```
